32 devices in a mesh: groups: 2 (over y), dp: 4 (over z), mp: 2 (over x), sub: 2 (over core).
Axes of the slice: x: 2, y: 2, z: 4, core: 2. Of those that a mesh axis runs over, the one named last changes fastest.
Arguments:
- context: bfloat16 [8, 256, 3072], P('groups', 'dp', ('mp', 'sub')), parts along dimension 0, may hold values from -8 to 8
- resid: bfloat16 [8, 256, 6144], P('groups', 'dp', ('mp', 'sub')), parts along dimension 0, may hold values from -60 to 60
- w_out: bfloat16 [3072, 6144], P('dp', ('mp', 'sub')), may hold values from -0.109375 to 0.109375
- b_out: float32 [6144], P(('mp', 'sub')), may hold values from -3 to 3
- ln_gain: float32 [6144], replicated, may hold values from 0.1 to 1.9
- w_proj: bfloat16 [6144, 4096], P('dp', ('mp', 'sub')), may hold values from -0.078125 to 0.078125
Outputs:
- projected: bfloat16 [8, 256, 4096], P(('groups', 'dp'), None, ('mp', 'sub')), parts along dimension 0
The draws below stay inside these ranges and needn't reach their ends.
There are 2 independent parts, one for each index of `groups`. The reference program is written for one: setup_inputs(seed, part) draws one part's arguments, and reference() takes and returns one part's arrays. A program takes and returns all parts, laid end to end along the dimension named above; an argument that names none is the same for every part. Nothing has to cross between parts.
All inputs are finite; a program needn't handle non-finite values.
Results may differ from the reference program's by a relative error of at most 0.0057.
Values may be sent and summed in bfloat16 or wider, within the bound.
No kernel may reach another device: no remote copies, remote signals or barrier semaphores. Data moves between devices by JAX's collectives and lax.ppermute only.
A program may use at most 128 MiB of HBM per device.

```python
import math
import jax
import jax.numpy as jnp
from jax import lax

D = 6144
F = 4096
PATCHES = 256
HD = 3072
IMAGES = 4


def draw_resid(key, part):
    key = jax.random.fold_in(key, 11)
    key_rows, key_jitter, key_base = jax.random.split(key, 3)
    row_scale = jnp.exp(jax.random.uniform(key_rows, (IMAGES, PATCHES, 1), jnp.float32, math.log(0.3), math.log(3.0)))
    ramp = jnp.exp(jnp.linspace(0.0, math.log(3.0), D)).astype(jnp.float32)
    jitter = jnp.exp(jax.random.uniform(key_jitter, (D,), jnp.float32, -0.35, 0.35))
    base = jnp.clip(jax.random.normal(key_base, (IMAGES, PATCHES, D), jnp.float32), -4.0, 4.0)
    return (base * row_scale * ramp * jitter).astype(jnp.bfloat16)


def steps_of(key, shape, shards, least, high):
    level, own = 1.0, jax.random.fold_in(key, 6)
    for dim, parts in shards:
        draws = jnp.exp(jax.random.uniform(jax.random.fold_in(own, dim), (parts,), jnp.float32, least / len(shards), high / len(shards)))
        level = level * jnp.repeat(draws, shape[dim] // parts).reshape([-1 if axis == dim else 1 for axis in range(len(shape))])
    return level


def scatter_about(rng, shape, scale, limit, shards=(), dtype=jnp.bfloat16):
    array = jax.random.normal(rng, shape, jnp.float32) * scale
    if len(shards) > 0:
        array = steps_of(rng, shape, shards, -0.22, 0.18) * array
    return jnp.clip(array, min=-limit, max=limit).astype(dtype)


def setup_inputs(seed: int = 0, part: int = 0) -> dict:
    splits = jax.random.split(jax.random.key(seed), 7)
    part_splits = jax.random.split(jax.random.fold_in(splits[6], part), 7)
    context = scatter_about(part_splits[0], (IMAGES, PATCHES, HD), 2.0, 8.0, ((1, 4), (2, 4)))
    resid = draw_resid(jax.random.fold_in(jax.random.fold_in(splits[6], part), 71), part)
    w_out = scatter_about(splits[2], (HD, D), HD ** -0.5, 0.109375, ((0, 4), (1, 4)))
    b_out = scatter_about(splits[3], (D,), 0.5, 3.0, ((0, 4),), jnp.float32)
    ln_gain = jnp.clip(1.0 + 0.18 * jax.random.normal(splits[4], (D,), jnp.float32), 0.1, 1.9)
    w_proj = scatter_about(splits[5], (D, F), D ** -0.5, 0.078125, ((0, 4), (1, 4)))
    return dict(context=context, resid=resid, w_out=w_out, b_out=b_out, ln_gain=ln_gain, w_proj=w_proj)


def reference(context, resid, w_out, b_out, ln_gain, w_proj):
    rows = context.reshape(-1, HD)
    attended = jnp.dot(rows, w_out, preferred_element_type=jnp.float32) + b_out
    summed = (resid.reshape(-1, D).astype(jnp.float32) + attended).astype(jnp.bfloat16)
    floats = lax.optimization_barrier(summed).astype(jnp.float32)
    center = lax.optimization_barrier(jnp.mean(floats, axis=-1, keepdims=True))
    spread = lax.optimization_barrier(jnp.mean(jnp.square(floats - center), axis=-1, keepdims=True))
    normed = ((floats - center) * lax.rsqrt(spread + 1e-06) * ln_gain).astype(jnp.bfloat16)
    projected = jnp.dot(normed, w_proj, preferred_element_type=jnp.float32).astype(jnp.bfloat16)
    return projected.reshape(IMAGES, PATCHES, F)
```

```python
import jax
import jax.numpy as jnp
from jax import lax
from jax.sharding import PartitionSpec as P

EPS = 1e-06
CHUNKS = 1


def normalize(values, ln_gain):
    floats = lax.optimization_barrier(values).astype(jnp.float32)
    shard_cols = values.shape[2]
    full_width = shard_cols * lax.axis_size(("mp", "sub"))
    totals, squares = lax.psum(
        (jnp.sum(floats, axis=-1, keepdims=True), jnp.sum(floats * floats, axis=-1, keepdims=True)),
        ("mp", "sub"),
    )
    center = totals / full_width
    spread = squares / full_width - center * center
    gain_share = lax.dynamic_slice_in_dim(
        ln_gain, lax.axis_index(("mp", "sub")) * shard_cols, shard_cols
    )
    shard_norm = ((floats - center) * lax.rsqrt(spread + EPS) * gain_share).astype(jnp.bfloat16)
    normed = lax.all_gather(shard_norm, ("mp", "sub"), axis=2, tiled=True)
    return normed.reshape(-1, normed.shape[2])


def project(normed, w_proj):
    summed_proj = jnp.dot(
        normed, lax.all_gather(w_proj, "dp", axis=0, tiled=True), preferred_element_type=jnp.float32
    )
    return summed_proj.astype(jnp.bfloat16)


def gathered(context, resid, w_out, b_out, ln_gain, w_proj):
    images, part_rows, head_cols = context.shape
    width_cols = resid.shape[2]
    tok_rows = context.reshape(images * part_rows, head_cols)
    heads_all = lax.all_gather(tok_rows, ("mp", "sub"), axis=1, tiled=True)
    attended = jnp.dot(
        heads_all,
        lax.all_gather(w_out, "dp", axis=0, tiled=True),
        preferred_element_type=jnp.float32,
    )
    summed = (resid.reshape(-1, width_cols).astype(jnp.float32) + attended + b_out).astype(
        jnp.bfloat16
    )
    summed = summed.reshape(images, part_rows, width_cols)
    moved = lax.all_to_all(summed, "dp", split_axis=0, concat_axis=1, tiled=True)
    normed = normalize(moved, ln_gain)
    return project(normed, w_proj).reshape(moved.shape[0], moved.shape[1], w_proj.shape[1])


GRID = ("dp", "mp", "sub")


def swap(value, step):
    count = lax.axis_size(("mp", "sub"))
    return lax.ppermute(value, ("mp", "sub"), [(a, a ^ step) for a in range(count)])


def turn(value, step, count):
    pairs = [
        (row * count + col, col * count + (row ^ col ^ step))
        for row in range(count)
        for col in range(count)
    ]
    return lax.ppermute(value, GRID, pairs)


def columns(value, sub):
    blocks = [value]
    while len(blocks) < lax.axis_size(("mp", "sub")):
        if len(blocks) < sub:
            blocks = blocks + [swap(b, len(blocks)) for b in blocks]
        else:
            far = swap(value, len(blocks))
            near = [far]
            while len(near) < len(blocks):
                near = near + [swap(b, len(near)) for b in near]
            blocks = blocks + near
    return blocks


def pick(stack, index):
    return lax.dynamic_index_in_dim(stack, index, 0, keepdims=False)


def stationary(context, resid, w_out, b_out, ln_gain, w_proj):
    count, sub = lax.axis_size("dp"), lax.axis_size("sub")
    row, col = lax.axis_index("dp"), lax.axis_index(("mp", "sub"))
    images, part_rows, head_cols = context.shape
    width_cols, out_cols = resid.shape[2], w_proj.shape[1]
    each = images // count
    patches = part_rows * count
    span = patches // CHUNKS

    by_image = context.reshape(count, each, part_rows, head_cols)
    came = jnp.stack([turn(pick(by_image, row ^ col ^ r), r, count) for r in range(count)])
    own = jnp.stack([pick(came, row ^ col ^ s) for s in range(count)], axis=1)
    own = own.reshape(each, patches, head_cols)
    heads = jnp.stack(columns(own, sub))

    gain = lax.dynamic_slice_in_dim(ln_gain, row * width_cols, width_cols)
    gain_proj = jnp.sum(gain[:, None] * w_proj.astype(jnp.float32), axis=0)
    gain_projs = lax.all_gather(gain_proj, "dp", axis=0)

    resid = resid.reshape(count, each, part_rows, width_cols)
    bias = jnp.where(row == 0, b_out, jnp.zeros_like(b_out))
    here = (jnp.arange(count) == row).reshape(1, count, 1, 1)

    sums = [0.0] * CHUNKS
    for c in range(CHUNKS):
        for r in range(count):
            rows = pick(heads, row ^ r)[:, c * span : (c + 1) * span]
            part = jnp.dot(
                rows.reshape(-1, head_cols), w_out, preferred_element_type=jnp.float32
            ).reshape(each, -1, part_rows, width_cols)
            mine = here[:, c * (span // part_rows) : (c + 1) * (span // part_rows)]
            old = pick(resid, row ^ col ^ r).astype(jnp.float32)[:, None]
            part = (part + bias + jnp.where(mine, old, 0.0)).astype(jnp.bfloat16)
            sums[c] = sums[c] + turn(part, r, count).astype(jnp.float32)

    outs = []
    for c in range(CHUNKS):
        summed = sums[c].astype(jnp.bfloat16).astype(jnp.float32).reshape(each * span, width_cols)
        mean = jnp.mean(summed, axis=1, keepdims=True)
        off = summed - mean
        square = jnp.sum(off * off, axis=1, keepdims=True)
        scaled = (off * gain).astype(jnp.bfloat16)
        stats = jnp.concatenate([mean, square], axis=1)
        stats = lax.ppermute(
            stats, GRID, [(a * count + b, b * count + a) for a in range(count) for b in range(count)]
        )
        stats = jnp.stack(columns(stats, sub))
        stats = jnp.stack([pick(stats, col ^ s) for s in range(count)])
        means, squares = stats[..., 0], stats[..., 1]
        center = jnp.mean(means, axis=0)
        shift = means - center
        spread = (jnp.sum(squares, axis=0) + width_cols * jnp.sum(shift * shift, axis=0)) / (
            width_cols * count
        )

        wide = jnp.stack(columns(scaled, sub))
        total = 0.0
        for e in reversed(range(count)):
            part = jnp.dot(pick(wide, row ^ e ^ col), w_proj, preferred_element_type=jnp.float32)
            if e:
                part = lax.ppermute(
                    part.astype(jnp.bfloat16), "dp", [(a, a ^ e) for a in range(count)]
                )
            total = total + part.astype(jnp.float32)
        fix = jnp.sum(shift[:, :, None] * gain_projs[:, None, :], axis=0)
        total = (total + fix) * lax.rsqrt(spread + EPS)[:, None]
        outs.append(total.astype(jnp.bfloat16).reshape(each, span, out_cols))
    return jnp.concatenate(outs, axis=1)


def local(context, *rest):
    count = lax.axis_size("dp")
    square = count == lax.axis_size(("mp", "sub")) and count & (count - 1) == 0
    whole = context.shape[0] % count == 0 and rest[1].shape[0] == context.shape[2]
    return (stationary if square and whole else gathered)(context, *rest)


def solution(mesh):
    in_specs = (
        P("groups", "dp", ("mp", "sub")),
        P("groups", "dp", ("mp", "sub")),
        P("dp", ("mp", "sub")),
        P(("mp", "sub")),
        P(),
        P("dp", ("mp", "sub")),
    )
    out_specs = P(("groups", "dp"), None, ("mp", "sub"))
    return jax.shard_map(local, mesh=mesh, in_specs=in_specs, out_specs=out_specs, check_vma=False)
```

```python
import jax
import jax.numpy as jnp
from jax import lax
from jax.sharding import PartitionSpec as P

EPS = 1e-06
CHUNKS = 2


def normalize(values, ln_gain):
    floats = lax.optimization_barrier(values).astype(jnp.float32)
    shard_cols = values.shape[2]
    full_width = shard_cols * lax.axis_size(("mp", "sub"))
    totals, squares = lax.psum(
        (jnp.sum(floats, axis=-1, keepdims=True), jnp.sum(floats * floats, axis=-1, keepdims=True)),
        ("mp", "sub"),
    )
    center = totals / full_width
    spread = squares / full_width - center * center
    gain_share = lax.dynamic_slice_in_dim(
        ln_gain, lax.axis_index(("mp", "sub")) * shard_cols, shard_cols
    )
    shard_norm = ((floats - center) * lax.rsqrt(spread + EPS) * gain_share).astype(jnp.bfloat16)
    normed = lax.all_gather(shard_norm, ("mp", "sub"), axis=2, tiled=True)
    return normed.reshape(-1, normed.shape[2])


def project(normed, w_proj):
    summed_proj = jnp.dot(
        normed, lax.all_gather(w_proj, "dp", axis=0, tiled=True), preferred_element_type=jnp.float32
    )
    return summed_proj.astype(jnp.bfloat16)


def gathered(context, resid, w_out, b_out, ln_gain, w_proj):
    images, part_rows, head_cols = context.shape
    width_cols = resid.shape[2]
    tok_rows = context.reshape(images * part_rows, head_cols)
    heads_all = lax.all_gather(tok_rows, ("mp", "sub"), axis=1, tiled=True)
    attended = jnp.dot(
        heads_all,
        lax.all_gather(w_out, "dp", axis=0, tiled=True),
        preferred_element_type=jnp.float32,
    )
    summed = (resid.reshape(-1, width_cols).astype(jnp.float32) + attended + b_out).astype(
        jnp.bfloat16
    )
    summed = summed.reshape(images, part_rows, width_cols)
    moved = lax.all_to_all(summed, "dp", split_axis=0, concat_axis=1, tiled=True)
    normed = normalize(moved, ln_gain)
    return project(normed, w_proj).reshape(moved.shape[0], moved.shape[1], w_proj.shape[1])


SWAP = [(0, 1), (1, 0)]
FOLD = [(0, 1), (3, 2)]
CROSS = [(1, 2), (2, 1)]
FAR = [(0, 2), (3, 1)]
SPREAD = [(1, 0), (2, 3)]
LEAP = [(1, 3), (2, 0)]


def along(value, axis, pairs):
    return lax.ppermute(value, axis, pairs)


def after(value, *earlier):
    return lax.optimization_barrier((value, *earlier))[0]


def pick(stack, index):
    return lax.dynamic_index_in_dim(stack, index, 0, keepdims=False)


def either(test, first, second):
    return jnp.where(test, first, second), jnp.where(test, second, first)


def centred(context, resid, w_out, b_out, ln_gain, w_proj):
    row, group = lax.axis_index("dp"), lax.axis_index("groups")
    x, core = lax.axis_index("mp"), lax.axis_index("sub")
    col = 2 * x + core
    low = row < 2
    images, part, heads = context.shape
    wide, out_cols = resid.shape[2], w_proj.shape[1]
    half = wide // 2
    span = part // CHUNKS
    tokens = images * 4 * span
    inner, outer = jnp.where(low, 0, half), jnp.where(low, half, 0)

    def cut(array, start, axis, size=half):
        return lax.dynamic_slice_in_dim(array, start, size, axis)

    def swapped(came):
        return jnp.concatenate(either(group == 0, came, along(came, "groups", SWAP)), axis=0)

    share = heads // 2
    out_outer, out_inner = cut(w_out, outer, 1), cut(w_out, inner, 1)
    fold_outer = along(cut(out_outer, group * share, 0, share), "dp", FOLD)

    kept, sent = either(x == 0, context[: images // 2], context[images // 2 :])
    first, second = either(x == 0, kept, along(sent, "mp", SWAP))
    near, away = either(low, first, second)
    mine = [along(near, "dp", FOLD), near, along(away, "dp", CROSS), along(away, "dp", FAR)]
    mine = jnp.where(low, jnp.stack(mine, 1), jnp.stack(mine[::-1], 1))

    old_outer, old_inner = cut(resid, outer, 2), cut(resid, inner, 2)
    came_outer = along(after(old_outer, fold_outer), "dp", FOLD)
    weight_outer = jnp.concatenate([swapped(fold_outer), out_outer], axis=0)

    fold_inner = along(after(cut(out_inner, group * share, 0, share), mine), "dp", FOLD)
    came_inner = along(after(old_inner, mine), "dp", FOLD)
    weight_inner = jnp.concatenate([swapped(fold_inner), out_inner], axis=0)

    share = half // 2
    proj_inner, proj_outer = cut(w_proj, inner, 0), cut(w_proj, outer, 0)
    sent_inner = cut(proj_inner, group * share, 0, share)
    sent_outer = cut(proj_outer, group * share, 0, share)
    proj_cross = along(after(sent_outer, mine), "dp", CROSS)
    proj_fold = along(after(sent_inner, fold_inner, came_inner), "dp", FOLD)
    proj_far = along(after(sent_outer, fold_inner, came_inner), "dp", FAR)
    slices = [swapped(proj_fold), proj_inner, swapped(proj_cross), swapped(proj_far)]
    slices = jnp.where(low, jnp.stack(slices), jnp.stack(slices[::-1]))
    slices = jnp.stack([pick(slices, col ^ d) for d in range(4)])
    gains = ln_gain.reshape(4, 2, half)
    gains = pick(gains.transpose(1, 0, 2), jnp.where(low, 0, 1))
    gains = jnp.stack([pick(gains, col ^ d) for d in range(4)])
    gain_proj = jnp.sum(gains[:, :, None] * slices.astype(jnp.float32), axis=1)

    bias = jnp.where(low, b_out, jnp.zeros_like(b_out))
    bias_outer, bias_inner = cut(bias, outer, 0), cut(bias, inner, 0)

    def attend(rows, weight, own, came, bias, k):
        own, came = (v[:, k * span : (k + 1) * span].astype(jnp.float32) for v in (own, came))
        none = jnp.zeros_like(own)
        old = jnp.where(
            low, jnp.stack([came, own, none, none], 1), jnp.stack([none, none, own, came], 1)
        )
        total = jnp.dot(rows, weight, preferred_element_type=jnp.float32)
        return total + old.reshape(tokens, half) + bias

    sums = []
    for k in range(CHUNKS):
        own = mine[:, :, k * span : (k + 1) * span]
        both = jnp.concatenate(either(x == 0, own, along(own, "mp", SWAP)), axis=0)
        both = both.reshape(tokens, heads)
        rows = jnp.concatenate(
            either(low == (core == 0), both, along(both, "sub", SWAP)), axis=1
        )
        sends = attend(rows, weight_outer, old_outer, came_outer, bias_outer, k)
        came = along(sends.astype(jnp.bfloat16), "dp", CROSS)
        keeps = attend(rows, weight_inner, old_inner, came_inner, bias_inner, k)
        sums.append((keeps + came.astype(jnp.float32)).astype(jnp.bfloat16))

    outs = []
    for k in range(CHUNKS):
        summed = sums[k].astype(jnp.float32)
        mean = jnp.mean(summed, axis=1)
        off = summed - mean[:, None]
        square = jnp.sum(off * off, axis=1)
        scaled = (off * gains[0]).astype(jnp.bfloat16)
        over = along(scaled, "mp", SWAP)
        all_scaled = [scaled, along(scaled, "sub", SWAP), over, along(over, "sub", SWAP)]

        stats = jnp.stack([mean, square])[None]
        stats = jnp.concatenate([stats, along(stats, "sub", SWAP)])
        stats = jnp.concatenate([stats, along(stats, "mp", SWAP)])
        middle = jnp.mean(stats[:, 0], axis=0)
        square = jnp.sum(stats[:, 1] + half * (stats[:, 0] - middle) ** 2, axis=0)
        there = along(jnp.stack([middle, square]), "dp", CROSS)
        center = 0.5 * (middle + there[0])
        gap = 0.5 * (middle - there[0])
        spread = (square + there[1]) / (8 * half) + gap * gap
        shift = stats[:, 0] - center
        scale = lax.rsqrt(spread + EPS)

        total = jnp.sum(shift[:, :, None] * gain_proj[:, None, :], axis=0)
        for d in range(4):
            total = total + jnp.dot(all_scaled[d], slices[d], preferred_element_type=jnp.float32)
        total = (total * scale[:, None]).reshape(images, 4 * span, out_cols)
        travel = total.astype(jnp.bfloat16)
        own = jnp.where((row == 1) | (row == 2), pick(total, row), 0.0)
        for pairs, image in (
            (LEAP, jnp.where(low, 3, 0)),
            (CROSS, jnp.where(low, 2, 1)),
            (SPREAD, jnp.where(low, 0, 3)),
        ):
            own = own + along(pick(travel, image), "dp", pairs).astype(jnp.float32)
        outs.append(own.astype(jnp.bfloat16).reshape(4, span, out_cols))
    return jnp.stack(outs, axis=1).reshape(1, 4 * part, out_cols)


def local(context, resid, w_out, b_out, ln_gain, w_proj):
    grid = [lax.axis_size(name) for name in ("groups", "dp", "mp", "sub")]
    fits = grid == [2, 4, 2, 2] and context.shape[0] == 4 and context.shape[1] % CHUNKS == 0
    plan = centred if fits else gathered
    return plan(context, resid, w_out, b_out, ln_gain, w_proj)


def solution(mesh):
    in_specs = (
        P("groups", "dp", ("mp", "sub")),
        P("groups", "dp", ("mp", "sub")),
        P("dp", ("mp", "sub")),
        P(("mp", "sub")),
        P(),
        P("dp", ("mp", "sub")),
    )
    out_specs = P(("groups", "dp"), None, ("mp", "sub"))
    return jax.shard_map(local, mesh=mesh, in_specs=in_specs, out_specs=out_specs, check_vma=False)
```

```python
import jax
import jax.numpy as jnp
from jax import lax
from jax.experimental import pallas as pl
from jax.experimental.pallas import tpu as pltpu
from jax.sharding import PartitionSpec as P

EPS = 1e-06
CHUNKS = 2


def normalize(values, ln_gain):
    floats = lax.optimization_barrier(values).astype(jnp.float32)
    shard_cols = values.shape[2]
    full_width = shard_cols * lax.axis_size(("mp", "sub"))
    totals, squares = lax.psum(
        (jnp.sum(floats, axis=-1, keepdims=True), jnp.sum(floats * floats, axis=-1, keepdims=True)),
        ("mp", "sub"),
    )
    center = totals / full_width
    spread = squares / full_width - center * center
    gain_share = lax.dynamic_slice_in_dim(
        ln_gain, lax.axis_index(("mp", "sub")) * shard_cols, shard_cols
    )
    shard_norm = ((floats - center) * lax.rsqrt(spread + EPS) * gain_share).astype(jnp.bfloat16)
    normed = lax.all_gather(shard_norm, ("mp", "sub"), axis=2, tiled=True)
    return normed.reshape(-1, normed.shape[2])


def project(normed, w_proj):
    summed_proj = jnp.dot(
        normed, lax.all_gather(w_proj, "dp", axis=0, tiled=True), preferred_element_type=jnp.float32
    )
    return summed_proj.astype(jnp.bfloat16)


def gathered(context, resid, w_out, b_out, ln_gain, w_proj):
    images, part_rows, head_cols = context.shape
    width_cols = resid.shape[2]
    tok_rows = context.reshape(images * part_rows, head_cols)
    heads_all = lax.all_gather(tok_rows, ("mp", "sub"), axis=1, tiled=True)
    attended = jnp.dot(
        heads_all,
        lax.all_gather(w_out, "dp", axis=0, tiled=True),
        preferred_element_type=jnp.float32,
    )
    summed = (resid.reshape(-1, width_cols).astype(jnp.float32) + attended + b_out).astype(
        jnp.bfloat16
    )
    summed = summed.reshape(images, part_rows, width_cols)
    moved = lax.all_to_all(summed, "dp", split_axis=0, concat_axis=1, tiled=True)
    normed = normalize(moved, ln_gain)
    return project(normed, w_proj).reshape(moved.shape[0], moved.shape[1], w_proj.shape[1])


SWAP = [(0, 1), (1, 0)]
FOLD = [(0, 1), (3, 2)]
CROSS = [(1, 2), (2, 1)]
FAR = [(0, 2), (3, 1)]
SPREAD = [(1, 0), (2, 3)]
LEAP = [(1, 3), (2, 0)]


def along(value, axis, pairs):
    return lax.ppermute(value, axis, pairs)


def pick(stack, index):
    return lax.dynamic_index_in_dim(stack, index, 0, keepdims=False)


def either(test, first, second):
    return jnp.where(test, first, second), jnp.where(test, second, first)


LIMIT = 48 * 1024 * 1024
ANY = pl.BlockSpec(memory_space=pl.ANY)
EXTRA = 16


def call(kernel, place, grid, ins, outs, shapes, scratch, args, flops=0):
    moved = sum(v.size * v.dtype.itemsize for v in (*args, *jax.tree.leaves(shapes)))
    return pl.pallas_call(
        kernel,
        grid_spec=pltpu.PrefetchScalarGridSpec(
            num_scalar_prefetch=1, grid=grid, in_specs=ins, out_specs=outs, scratch_shapes=scratch
        ),
        out_shape=shapes,
        compiler_params=pltpu.CompilerParams(vmem_limit_bytes=LIMIT),
        cost_estimate=pl.CostEstimate(flops=flops, bytes_accessed=moved, transcendentals=0),
    )(place, *args)


def cuts(place, blocks, *released):
    def kernel(place_ref, *refs):
        for src, dst in zip(refs[: len(blocks)], refs[-len(blocks) :]):
            dst[...] = src[...]

    def spec(block, index=None):
        return pl.BlockSpec(block, index or (lambda i, p: (0,) * len(block)))

    return call(
        kernel,
        place,
        (1,),
        [spec(block, index) for _, block, index in blocks] + [ANY] * len(released),
        [spec(block) for _, block, _ in blocks],
        [jax.ShapeDtypeStruct(block, array.dtype) for array, block, _ in blocks],
        [],
        [array for array, _, _ in blocks] + list(released),
    )


def terms(value):
    high = value.astype(jnp.bfloat16)
    rest = value - high.astype(jnp.float32)
    mid = rest.astype(jnp.bfloat16)
    return [high, mid, (rest - mid.astype(jnp.float32)).astype(jnp.bfloat16)]


def added(rows, first):
    high, mid, low = (rows[first + i : first + i + 1].astype(jnp.float32) for i in range(3))
    return high + (mid + low)


def packed(rows):
    parts = [term for row in rows for term in terms(row)]
    parts.append(jnp.zeros((EXTRA - len(parts), rows[0].shape[1]), jnp.bfloat16))
    return jnp.concatenate(parts, axis=0)


def upright(rows):
    rows = jnp.concatenate(rows, axis=0)
    fill = jnp.zeros((128 - rows.shape[0], rows.shape[1]), jnp.float32)
    return jnp.concatenate([rows, fill], axis=0).T


def attend(place, both, other, w_out, fold, swapped, resid, came, bias, part, inner, dtype):
    tokens, heads = both.shape
    half, share = fold.shape[1], fold.shape[0]
    images, span = resid.shape[0], tokens // resid.shape[0] // 4
    tile = 256 if half % 256 == 0 else half
    tiles = half // tile

    def kernel(p, both, other, own, fold, swapped, old, came, bias, out, total):
        low = p[0] == 1
        turn = low == (p[2] == 0)
        here = jnp.where(turn, other[...], both[...])
        folded = jnp.where(turn, both[...], other[...])
        first = jnp.where(p[1] == 0, fold[...], swapped[...])
        second = jnp.where(p[1] == 0, swapped[...], fold[...])
        value = jnp.dot(here, own[...], preferred_element_type=jnp.float32)
        value = value + jnp.dot(folded[:, :share], first, preferred_element_type=jnp.float32)
        value = value + jnp.dot(folded[:, share:], second, preferred_element_type=jnp.float32)
        total[...] = value + jnp.where(low, bias[...], jnp.zeros_like(bias[...]))
        own_at, came_at = jnp.where(low, span, 2 * span), jnp.where(low, 0, 3 * span)
        for image in range(images):
            for at, source in ((own_at, old), (came_at, came)):
                rows = pl.ds(pl.multiple_of(image * 4 * span + at, span), span)
                total[rows, :] = total[rows, :] + source[image].astype(jnp.float32)
        out[...] = total[...].astype(dtype)

    def column(p, t):
        return jnp.where((p[0] == 1) == inner, 0, tiles) + t

    whole = pl.BlockSpec((tokens, heads), lambda t, p: (0, 0))
    piece = pl.BlockSpec((share, tile), lambda t, p: (0, t))
    return call(
        kernel,
        place,
        (tiles,),
        [
            whole,
            whole,
            pl.BlockSpec((heads, tile), lambda t, p: (0, column(p, t))),
            piece,
            piece,
            pl.BlockSpec((images, span, tile), lambda t, p: (0, part, column(p, t))),
            pl.BlockSpec((images, span, tile), lambda t, p: (0, part, t)),
            pl.BlockSpec((1, tile), lambda t, p: (0, column(p, t))),
        ],
        pl.BlockSpec((tokens, tile), lambda t, p: (0, t)),
        jax.ShapeDtypeStruct((tokens, half), dtype),
        [pltpu.VMEM((tokens, tile), jnp.float32)],
        [both, other, w_out, fold, swapped, resid, came, bias.reshape(1, -1)],
        flops=4 * tokens * heads * half,
    )


def scale_up(place, keeps, came, gain):
    tokens, half = keeps.shape

    def kernel(p, keeps, came, gain, out):
        step = pl.program_id(0)
        summed = (keeps[...] + came[...].astype(jnp.float32)).astype(jnp.bfloat16)
        summed = summed.astype(jnp.float32)
        mean = jnp.sum(summed, axis=1, keepdims=True) / half
        off = summed - mean
        square = jnp.sum(off * off, axis=1, keepdims=True)
        at = pl.multiple_of(step * 128, 128)
        out[pl.ds(at, 128), :] = (off * gain[...]).astype(jnp.bfloat16)
        lane = lax.broadcasted_iota(jnp.int32, (128, 128), 1)
        stats = jnp.where(lane == 0, mean, jnp.where(lane == 1, square, 0.0)).T
        out[tokens:, pl.ds(at, 128)] = packed([stats[0:1], stats[1:2]])

    row = pl.BlockSpec((128, half), lambda i, p: (i, 0))
    return call(
        kernel,
        place,
        (tokens // 128,),
        [row, row, pl.BlockSpec((1, half), lambda i, p: (0, 0))],
        pl.BlockSpec((tokens + EXTRA, half), lambda i, p: (0, 0)),
        jax.ShapeDtypeStruct((tokens + EXTRA, half), jnp.bfloat16),
        [],
        [keeps, came, gain],
    )


def project_up(place, scaled, slices, gain_proj):
    rows, half = scaled[0].shape
    tokens, out_cols = rows - EXTRA, slices.shape[1]
    size = tokens // 4
    tile = 256 if out_cols % 256 == 0 else out_cols

    def kernel(p, s0, s1, s2, s3, slices, gain_proj, o0, o1, o2, o3, shifts, stats, total):
        @pl.when(pl.program_id(0) == 0)
        def _():
            last = [s[tokens:, :tokens] for s in (s0, s1, s2, s3)]
            means = [added(v, 0) for v in last]
            middle = 0.25 * (means[0] + means[1] + means[2] + means[3])
            shift = [v - middle for v in means]
            square = sum(added(v, 3) + half * (d * d) for v, d in zip(last, shift))
            shifts[...] = upright(shift)
            for image in range(4):
                at = slice(image * size, (image + 1) * size)
                stats[image] = jnp.concatenate([middle[:, at], square[:, at]], axis=0)

        value = jnp.zeros(total.shape, jnp.float32)
        for d, s in enumerate((s0, s1, s2, s3)):
            value = value + jnp.dot(
                s[:tokens, :],
                slices[d * half : (d + 1) * half, :],
                preferred_element_type=jnp.float32,
            )
            value = value + shifts[:, d : d + 1] * gain_proj[d : d + 1, :]
        total[...] = value
        gains = jnp.sum(gain_proj[...], axis=0, keepdims=True)
        for role, out in enumerate((o0, o1, o2, o3)):
            image = jnp.where(p[0] == 1, role, 3 - role)
            at = pl.ds(pl.multiple_of(image * size, size), size)
            out[:size, :] = total[at, :].astype(jnp.bfloat16)
            here = stats[image]
            here = jnp.concatenate([here] * (gains.shape[1] // size), axis=1)
            out[size:, :] = packed([here[0:1], here[1:2], gains])

    whole = pl.BlockSpec((rows, half), lambda t, p: (0, 0))
    message = pl.BlockSpec((size + EXTRA, tile), lambda t, p: (0, t))
    return call(
        kernel,
        place,
        (out_cols // tile,),
        [whole] * 4
        + [
            pl.BlockSpec((4 * half, tile), lambda t, p: (0, t)),
            pl.BlockSpec((4, tile), lambda t, p: (0, t)),
        ],
        [message] * 4,
        [jax.ShapeDtypeStruct((size + EXTRA, out_cols), jnp.bfloat16)] * 4,
        [
            pltpu.VMEM((tokens, 128), jnp.float32),
            pltpu.VMEM((4, 2, size), jnp.float32),
            pltpu.VMEM((tokens, tile), jnp.float32),
        ],
        [*scaled, slices, gain_proj],
        flops=8 * tokens * half * out_cols,
    )


def finish(place, parts, count):
    rows, out_cols = parts[0][0].shape
    size = rows - EXTRA
    span = size // 4

    def kernel(p, *refs):
        out = refs[-1]
        middle = (p[3] == 1) | (p[3] == 2)
        for k in range(len(parts)):
            own, cross, spread, leap = refs[4 * k : 4 * k + 4]
            one = jnp.where(middle, own[...], spread[...])
            two = jnp.where(middle, cross[...], leap[...])
            ends = [one[size:], two[size:]]
            means = [added(v, 0)[:, :size] for v in ends]
            squares = [added(v, 3)[:, :size] for v in ends]
            gap = 0.5 * (means[0] - means[1])
            spread_of = (squares[0] + squares[1]) / count + gap * gap
            turned = upright([gap, lax.rsqrt(spread_of + EPS)])
            value = one[:size].astype(jnp.float32) + two[:size].astype(jnp.float32)
            value = value + turned[:, 0:1] * (added(ends[0], 6) - added(ends[1], 6))
            value = (value * turned[:, 1:2]).astype(jnp.bfloat16)
            for row in range(4):
                at = (row * len(parts) + k) * span
                out[at : at + span, :] = value[row * span : (row + 1) * span]

    args = [v for part in parts for v in part]
    return call(
        kernel,
        place,
        (1,),
        [pl.BlockSpec((rows, out_cols), lambda i, p: (0, 0))] * len(args),
        pl.BlockSpec((size * len(parts), out_cols), lambda i, p: (0, 0)),
        jax.ShapeDtypeStruct((size * len(parts), out_cols), jnp.bfloat16),
        [],
        args,
    )


def centred(context, resid, w_out, b_out, ln_gain, w_proj):
    row, group = lax.axis_index("dp"), lax.axis_index("groups")
    x, core = lax.axis_index("mp"), lax.axis_index("sub")
    col = 2 * x + core
    low = row < 2
    place = jnp.stack([low.astype(jnp.int32), group, core, row])
    images, part, heads = context.shape
    wide, out_cols = resid.shape[2], w_proj.shape[1]
    half = wide // 2
    span = part // CHUNKS

    def halves(came, swap):
        return jnp.concatenate(either(group == 0, came, swap), axis=0)

    def inner(p):
        return 1 - p[0]

    def outer(p):
        return p[0]

    share, share2 = heads // 2, half // 2
    sent_outer, sent_cross = cuts(
        place,
        [
            (w_out, (share, half), lambda i, p: (p[1], outer(p))),
            (w_proj, (share2, out_cols), lambda i, p: (2 * outer(p) + p[1], 0)),
        ],
    )
    kept, sent = either(x == 0, context[: images // 2], context[images // 2 :])
    got = along(sent, "mp", SWAP)
    fold_outer = along(sent_outer, "dp", FOLD)
    proj_cross = along(sent_cross, "dp", CROSS)

    first, second = either(x == 0, kept, got)
    near, away = either(low, first, second)
    mine = [along(near, "dp", FOLD), near, along(away, "dp", CROSS), along(away, "dp", FAR)]
    mine = jnp.where(low, jnp.stack(mine, 1), jnp.stack(mine[::-1], 1))

    old = (images, part, half)
    sent_inner, sent_old = cuts(
        place,
        [
            (w_out, (share, half), lambda i, p: (p[1], inner(p))),
            (resid, old, lambda i, p: (0, 0, outer(p))),
        ],
        got,
    )
    old_outer = along(sent_old, "dp", FOLD)
    fold_inner = along(sent_inner, "dp", FOLD)
    swap_outer = along(fold_outer, "groups", SWAP)
    swap_inner = along(fold_inner, "groups", SWAP)

    sent_fold, sent_old = cuts(
        place,
        [
            (w_proj, (share2, out_cols), lambda i, p: (2 * inner(p) + p[1], 0)),
            (resid, old, lambda i, p: (0, 0, inner(p))),
        ],
        mine,
    )
    old_inner = along(sent_old, "dp", FOLD)
    proj_fold = along(sent_fold, "dp", FOLD)
    (sent_far,) = cuts(
        place,
        [(w_proj, (share2, out_cols), lambda i, p: (2 * outer(p) + p[1], 0))],
        fold_inner,
    )
    proj_far = along(sent_far, "dp", FAR)

    sends, keeps = [], []
    for k in range(CHUNKS):
        own = mine[:, :, k * span : (k + 1) * span]
        both = jnp.concatenate(either(x == 0, own, along(own, "mp", SWAP)), axis=0)
        both = both.reshape(images * 4 * span, heads)
        other = along(both, "sub", SWAP)
        common = (place, both, other, w_out)
        sends.append(
            attend(*common, fold_outer, swap_outer, resid, old_outer, b_out, k, False, jnp.bfloat16)
        )
        keeps.append(
            attend(*common, fold_inner, swap_inner, resid, old_inner, b_out, k, True, jnp.float32)
        )

    gains = ln_gain.reshape(4, 2, half)
    gains = pick(gains.transpose(1, 0, 2), jnp.where(low, 0, 1))
    gains = jnp.stack([pick(gains, col ^ d) for d in range(4)])
    came = [along(v, "dp", CROSS) for v in sends]
    scaled = []
    for k in range(CHUNKS):
        near = scale_up(place, keeps[k], came[k], gains[:1])
        far = along(near, "mp", SWAP)
        scaled.append([near, along(near, "sub", SWAP), far, along(far, "sub", SWAP)])

    proj_own = lax.dynamic_slice_in_dim(w_proj, jnp.where(low, 0, half), half, 0)
    slices = [
        halves(proj_fold, along(proj_fold, "groups", SWAP)),
        proj_own,
        halves(proj_cross, along(proj_cross, "groups", SWAP)),
        halves(proj_far, along(proj_far, "groups", SWAP)),
    ]
    slices = jnp.where(low, jnp.stack(slices), jnp.stack(slices[::-1]))
    slices = jnp.stack([pick(slices, col ^ d) for d in range(4)])
    gain_proj = jnp.sum(gains[:, :, None] * slices.astype(jnp.float32), axis=1)
    slices = slices.reshape(4 * half, out_cols)

    parts = []
    for k in range(CHUNKS):
        spread, own, cross, leap = project_up(place, scaled[k], slices, gain_proj)
        leap = along(leap, "dp", LEAP)
        cross = along(cross, "dp", CROSS)
        spread = along(spread, "dp", SPREAD)
        parts.append([own, cross, spread, leap])
    return finish(place, parts, 8 * half).reshape(1, 4 * part, out_cols)


def local(context, resid, w_out, b_out, ln_gain, w_proj):
    grid = [lax.axis_size(name) for name in ("groups", "dp", "mp", "sub")]
    fits = grid == [2, 4, 2, 2] and context.shape[0] == 4 and context.shape[1] % CHUNKS == 0
    plan = centred if fits else gathered
    return plan(context, resid, w_out, b_out, ln_gain, w_proj)


def solution(mesh):
    in_specs = (
        P("groups", "dp", ("mp", "sub")),
        P("groups", "dp", ("mp", "sub")),
        P("dp", ("mp", "sub")),
        P(("mp", "sub")),
        P(),
        P("dp", ("mp", "sub")),
    )
    out_specs = P(("groups", "dp"), None, ("mp", "sub"))
    return jax.shard_map(local, mesh=mesh, in_specs=in_specs, out_specs=out_specs, check_vma=False)
```

```python
import jax
import jax.numpy as jnp
from jax import lax
from jax.experimental import pallas as pl
from jax.experimental.pallas import tpu as pltpu
from jax.sharding import PartitionSpec as P

EPS = 1e-06
CHUNKS = 2


def normalize(values, ln_gain):
    floats = lax.optimization_barrier(values).astype(jnp.float32)
    shard_cols = values.shape[2]
    full_width = shard_cols * lax.axis_size(("mp", "sub"))
    totals, squares = lax.psum(
        (jnp.sum(floats, axis=-1, keepdims=True), jnp.sum(floats * floats, axis=-1, keepdims=True)),
        ("mp", "sub"),
    )
    center = totals / full_width
    spread = squares / full_width - center * center
    gain_share = lax.dynamic_slice_in_dim(
        ln_gain, lax.axis_index(("mp", "sub")) * shard_cols, shard_cols
    )
    shard_norm = ((floats - center) * lax.rsqrt(spread + EPS) * gain_share).astype(jnp.bfloat16)
    normed = lax.all_gather(shard_norm, ("mp", "sub"), axis=2, tiled=True)
    return normed.reshape(-1, normed.shape[2])


def project(normed, w_proj):
    summed_proj = jnp.dot(
        normed, lax.all_gather(w_proj, "dp", axis=0, tiled=True), preferred_element_type=jnp.float32
    )
    return summed_proj.astype(jnp.bfloat16)


def gathered(context, resid, w_out, b_out, ln_gain, w_proj):
    images, part_rows, head_cols = context.shape
    width_cols = resid.shape[2]
    tok_rows = context.reshape(images * part_rows, head_cols)
    heads_all = lax.all_gather(tok_rows, ("mp", "sub"), axis=1, tiled=True)
    attended = jnp.dot(
        heads_all,
        lax.all_gather(w_out, "dp", axis=0, tiled=True),
        preferred_element_type=jnp.float32,
    )
    summed = (resid.reshape(-1, width_cols).astype(jnp.float32) + attended + b_out).astype(
        jnp.bfloat16
    )
    summed = summed.reshape(images, part_rows, width_cols)
    moved = lax.all_to_all(summed, "dp", split_axis=0, concat_axis=1, tiled=True)
    normed = normalize(moved, ln_gain)
    return project(normed, w_proj).reshape(moved.shape[0], moved.shape[1], w_proj.shape[1])


SWAP = [(0, 1), (1, 0)]
FOLD = [(0, 1), (3, 2)]
CROSS = [(1, 2), (2, 1)]
FAR = [(0, 2), (3, 1)]
SPREAD = [(1, 0), (2, 3)]
LEAP = [(1, 3), (2, 0)]


def along(value, axis, pairs):
    return lax.ppermute(value, axis, pairs)


def pick(stack, index):
    return lax.dynamic_index_in_dim(stack, index, 0, keepdims=False)


def either(test, first, second):
    return jnp.where(test, first, second), jnp.where(test, second, first)


LIMIT = 48 * 1024 * 1024
ANY = pl.BlockSpec(memory_space=pl.ANY)
EXTRA = 16


def call(kernel, place, grid, ins, outs, shapes, scratch, args):
    return pl.pallas_call(
        kernel,
        grid_spec=pltpu.PrefetchScalarGridSpec(
            num_scalar_prefetch=1, grid=grid, in_specs=ins, out_specs=outs, scratch_shapes=scratch
        ),
        out_shape=shapes,
        compiler_params=pltpu.CompilerParams(vmem_limit_bytes=LIMIT),
        cost_estimate=pl.CostEstimate(flops=1, bytes_accessed=1, transcendentals=0),
    )(place, *args)


def cuts(place, blocks, *released):
    def kernel(place_ref, *refs):
        for src, dst in zip(refs[: len(blocks)], refs[-len(blocks) :]):
            dst[...] = src[...]

    def spec(block, index=None):
        return pl.BlockSpec(block, index or (lambda i, p: (0,) * len(block)))

    return call(
        kernel,
        place,
        (1,),
        [spec(block, index) for _, block, index in blocks] + [ANY] * len(released),
        [spec(block) for _, block, _ in blocks],
        [jax.ShapeDtypeStruct(block, array.dtype) for array, block, _ in blocks],
        [],
        [array for array, _, _ in blocks] + list(released),
    )


def terms(value):
    high = value.astype(jnp.bfloat16)
    rest = value - high.astype(jnp.float32)
    mid = rest.astype(jnp.bfloat16)
    return [high, mid, (rest - mid.astype(jnp.float32)).astype(jnp.bfloat16)]


def added(rows, first):
    high, mid, low = (rows[first + i : first + i + 1].astype(jnp.float32) for i in range(3))
    return high + (mid + low)


def packed(rows):
    parts = [term for row in rows for term in terms(row)]
    parts.append(jnp.zeros((EXTRA - len(parts), rows[0].shape[1]), jnp.bfloat16))
    return jnp.concatenate(parts, axis=0)


def upright(rows):
    rows = jnp.concatenate(rows, axis=0)
    fill = jnp.zeros((128 - rows.shape[0], rows.shape[1]), jnp.float32)
    return jnp.concatenate([rows, fill], axis=0).T


def attend(place, tokens_of, w_out, fold, swapped, resid, came, bias, part, inner, dtype):
    rows, heads = tokens_of[0].shape
    tokens = 2 * rows
    half, share = fold.shape[1], fold.shape[0]
    images, span = resid.shape[0], tokens // resid.shape[0] // 4
    tile = 256 if half % 256 == 0 else half
    tiles = half // tile

    def kernel(p, own, far, near, both, weight, fold, swapped, old, came, bias, out, left, total):
        low = p[0] == 1
        turn = low == (p[2] == 0)

        @pl.when(pl.program_id(0) == 0)
        def _():
            for at, one, two in ((p[5], own, near), (1 - p[5], far, both)):
                at = pl.ds(pl.multiple_of(at * rows, rows), rows)
                left[at, :heads] = jnp.where(turn, two[...], one[...])
                folded = jnp.where(turn, one[...], two[...])
                first, second = folded[:, :share], folded[:, share:]
                left[at, heads : heads + share] = jnp.where(p[1] == 0, first, second)
                left[at, heads + share :] = jnp.where(p[1] == 0, second, first)

        value = jnp.dot(left[:, :heads], weight[...], preferred_element_type=jnp.float32)
        for i, piece in enumerate((fold, swapped)):
            at = slice(heads + i * share, heads + (i + 1) * share)
            value = value + jnp.dot(left[:, at], piece[...], preferred_element_type=jnp.float32)
        total[...] = value + jnp.where(low, bias[...], jnp.zeros_like(bias[...]))
        own_at, came_at = jnp.where(low, span, 2 * span), jnp.where(low, 0, 3 * span)
        for image in range(images):
            for at, source in ((own_at, old), (came_at, came)):
                at = pl.ds(pl.multiple_of(image * 4 * span + at, span), span)
                total[at, :] = total[at, :] + source[image].astype(jnp.float32)
        out[...] = total[...].astype(dtype)

    def column(p, t):
        return jnp.where((p[0] == 1) == inner, 0, tiles) + t

    whole = pl.BlockSpec((rows, heads), lambda t, p: (0, 0))
    piece = pl.BlockSpec((share, tile), lambda t, p: (0, t))
    return call(
        kernel,
        place,
        (tiles,),
        [whole] * 4
        + [
            pl.BlockSpec((heads, tile), lambda t, p: (0, column(p, t))),
            piece,
            piece,
            pl.BlockSpec((images, span, tile), lambda t, p: (0, part, column(p, t))),
            pl.BlockSpec((images, span, tile), lambda t, p: (0, part, t)),
            pl.BlockSpec((1, tile), lambda t, p: (0, column(p, t))),
        ],
        pl.BlockSpec((tokens, tile), lambda t, p: (0, t)),
        jax.ShapeDtypeStruct((tokens, half), dtype),
        [pltpu.VMEM((tokens, 2 * heads), jnp.bfloat16), pltpu.VMEM((tokens, tile), jnp.float32)],
        [*tokens_of, w_out, fold, swapped, resid, came, bias],
    )


def scale_up(place, keeps, came, gain):
    tokens, half = keeps.shape

    def kernel(p, keeps, came, gain, out):
        step = pl.program_id(0)
        summed = (keeps[...] + came[...].astype(jnp.float32)).astype(jnp.bfloat16)
        summed = summed.astype(jnp.float32)
        mean = jnp.sum(summed, axis=1, keepdims=True) / half
        off = summed - mean
        square = jnp.sum(off * off, axis=1, keepdims=True)
        at = pl.multiple_of(step * 128, 128)
        out[pl.ds(at, 128), :] = (off * gain[...]).astype(jnp.bfloat16)
        lane = lax.broadcasted_iota(jnp.int32, (128, 128), 1)
        stats = jnp.where(lane == 0, mean, jnp.where(lane == 1, square, 0.0)).T
        out[tokens:, pl.ds(at, 128)] = packed([stats[0:1], stats[1:2]])

    row = pl.BlockSpec((128, half), lambda i, p: (i, 0))
    return call(
        kernel,
        place,
        (tokens // 128,),
        [row, row, pl.BlockSpec((1, half), lambda i, p: (0, 2 * p[4] + 1 - p[0]))],
        pl.BlockSpec((tokens + EXTRA, half), lambda i, p: (0, 0)),
        jax.ShapeDtypeStruct((tokens + EXTRA, half), jnp.bfloat16),
        [],
        [keeps, came, gain],
    )


def project_up(place, scaled, w_proj, pieces, gain):
    rows, half = scaled[0].shape
    tokens, out_cols = rows - EXTRA, w_proj.shape[1]
    size, share = tokens // 4, half // 2
    tile = 256 if out_cols % 256 == 0 else out_cols

    def kernel(p, s0, s1, s2, s3, own, f0, f1, c0, c1, a0, a1, gain, *rest):
        outs, (left, shifts, stats, total) = rest[:4], rest[4:]
        low = p[0] == 1

        def slot(feature):
            return jnp.where(low, feature, 3 - feature)

        def put(value, at, rows):
            swap = (p[1] == 1) & (at != 1)
            first, second = value[:, :share], value[:, share:]
            left[at, rows, :share] = jnp.where(swap, second, first)
            left[at, rows, share:] = jnp.where(swap, first, second)

        @pl.when(pl.program_id(0) == 0)
        def _():
            last = [s[tokens:, :tokens] for s in (s0, s1, s2, s3)]
            means = [added(v, 0) for v in last]
            middle = 0.25 * (means[0] + means[1] + means[2] + means[3])
            shift = [v - middle for v in means]
            square = sum(added(v, 3) + half * (d * d) for v, d in zip(last, shift))
            for image in range(4):
                at = slice(image * size, (image + 1) * size)
                stats[image] = jnp.concatenate([middle[:, at], square[:, at]], axis=0)
            for d, s in enumerate((s0, s1, s2, s3)):
                feature = p[4] ^ d
                put(s[:tokens, :], slot(feature), slice(0, tokens))
                at = pl.multiple_of((2 * feature + 1 - p[0]) * half, half)
                put(packed([gain[:, pl.ds(at, half)]]), slot(feature), slice(tokens, rows))
            turned = upright(shift).astype(jnp.float32)
            high, mid, low_term = terms(turned)
            zero = jnp.zeros((tokens, 128), jnp.bfloat16)
            lane = lax.broadcasted_iota(jnp.int32, (tokens, 128), 1)
            spread = zero
            for d in range(4):
                for i, term in enumerate((high, high, high, mid, mid, low_term)):
                    spread = jnp.where(lane == 6 * d + i, term[:, d : d + 1], spread)
            shifts[...] = spread

        value = jnp.zeros((rows, tile), jnp.float32)
        gains = []
        for at, halves in enumerate(((f0, f1), (own,), (c0, c1), (a0, a1))):
            piece = jnp.zeros((rows, tile), jnp.float32)
            for i, weight in enumerate(halves):
                depth = weight.shape[0]
                piece = piece + jnp.dot(
                    left[at, :, i * depth : (i + 1) * depth],
                    weight[...],
                    preferred_element_type=jnp.float32,
                )
            value = value + piece
            gains.append(jnp.sum(piece[tokens : tokens + 3], axis=0, keepdims=True))
        fix = []
        for d in range(4):
            at = slot(p[4] ^ d)
            row = sum(jnp.where(at == i, gains[i], 0.0) for i in range(4))
            high, mid, low_term = terms(row)
            fix += [high, mid, low_term, high, mid, high]
        fix.append(jnp.zeros((128 - len(fix), tile), jnp.bfloat16))
        fix = jnp.dot(
            shifts[...], jnp.concatenate(fix, axis=0), preferred_element_type=jnp.float32
        )
        total[...] = value[:tokens] + fix
        gains = gains[0] + gains[1] + gains[2] + gains[3]
        for role, out in enumerate(outs):
            image = jnp.where(low, role, 3 - role)
            at = pl.ds(pl.multiple_of(image * size, size), size)
            out[:size, :] = total[at, :].astype(jnp.bfloat16)
            here = stats[image]
            here = jnp.concatenate([here] * (tile // size), axis=1)
            out[size:, :] = packed([here[0:1], here[1:2], gains])

    whole = pl.BlockSpec((rows, half), lambda t, p: (0, 0))
    message = pl.BlockSpec((size + EXTRA, tile), lambda t, p: (0, t))
    piece = pl.BlockSpec((share, tile), lambda t, p: (0, t))
    return call(
        kernel,
        place,
        (out_cols // tile,),
        [whole] * 4
        + [pl.BlockSpec((half, tile), lambda t, p: (1 - p[0], t))]
        + [piece] * 6
        + [pl.BlockSpec(gain.shape, lambda t, p: (0, 0))],
        [message] * 4,
        [jax.ShapeDtypeStruct((size + EXTRA, out_cols), jnp.bfloat16)] * 4,
        [
            pltpu.VMEM((4, rows, half), jnp.bfloat16),
            pltpu.VMEM((tokens, 128), jnp.bfloat16),
            pltpu.VMEM((4, 2, size), jnp.float32),
            pltpu.VMEM((tokens, tile), jnp.float32),
        ],
        [*scaled, w_proj, *pieces, gain],
    )


def finish(place, parts, count):
    rows, out_cols = parts[0][0].shape
    size = rows - EXTRA
    span = size // 4

    def kernel(p, *refs):
        out = refs[-1]
        middle = (p[3] == 1) | (p[3] == 2)
        for k in range(len(parts)):
            own, cross, spread, leap = refs[4 * k : 4 * k + 4]
            one = jnp.where(middle, own[...], spread[...])
            two = jnp.where(middle, cross[...], leap[...])
            ends = [one[size:], two[size:]]
            means = [added(v, 0)[:, :size] for v in ends]
            squares = [added(v, 3)[:, :size] for v in ends]
            gap = 0.5 * (means[0] - means[1])
            spread_of = (squares[0] + squares[1]) / count + gap * gap
            turned = upright([gap, lax.rsqrt(spread_of + EPS)])
            value = one[:size].astype(jnp.float32) + two[:size].astype(jnp.float32)
            value = value + turned[:, 0:1] * (added(ends[0], 6) - added(ends[1], 6))
            value = (value * turned[:, 1:2]).astype(jnp.bfloat16)
            for row in range(4):
                at = (row * len(parts) + k) * span
                out[at : at + span, :] = value[row * span : (row + 1) * span]

    args = [v for part in parts for v in part]
    return call(
        kernel,
        place,
        (1,),
        [pl.BlockSpec((rows, out_cols), lambda i, p: (0, 0))] * len(args),
        pl.BlockSpec((size * len(parts), out_cols), lambda i, p: (0, 0)),
        jax.ShapeDtypeStruct((size * len(parts), out_cols), jnp.bfloat16),
        [],
        args,
    )


def facing(place, context, got, block, *released):
    array, shape, index = block
    images, part, heads = got.shape

    def kernel(p, kept, got, src, *refs):
        near, away, dst = refs[-3:]
        same = (p[0] == 1) == (p[5] == 0)
        near[...] = jnp.where(same, kept[...], got[...])
        away[...] = jnp.where(same, got[...], kept[...])
        dst[...] = src[...]

    whole = pl.BlockSpec(got.shape, lambda i, p: (0, 0, 0))
    return call(
        kernel,
        place,
        (1,),
        [pl.BlockSpec(got.shape, lambda i, p: (p[5], 0, 0)), whole]
        + [pl.BlockSpec(shape, index)]
        + [ANY] * len(released),
        [whole, whole, pl.BlockSpec(shape, lambda i, p: (0,) * len(shape))],
        [jax.ShapeDtypeStruct(got.shape, got.dtype)] * 2
        + [jax.ShapeDtypeStruct(shape, array.dtype)],
        [],
        [context, got, array, *released],
    )


def ordered(place, pieces, block, *released):
    array, shape, index = block
    images, part, heads = pieces[0].shape
    span = part // CHUNKS
    rows = images * 4 * span

    def kernel(p, *refs):
        ins, outs = refs[:4], refs[-CHUNKS - 1 : -1]
        for k, out in enumerate(outs):
            at = slice(k * span, (k + 1) * span)
            for image in range(images):
                for row in range(4):
                    to = (image * 4 + row) * span
                    out[to : to + span, :] = jnp.where(
                        p[0] == 1, ins[row][image, at, :], ins[3 - row][image, at, :]
                    )
        refs[-1][...] = refs[4][...]

    whole = pl.BlockSpec(pieces[0].shape, lambda i, p: (0, 0, 0))
    return call(
        kernel,
        place,
        (1,),
        [whole] * 4 + [pl.BlockSpec(shape, index)] + [ANY] * len(released),
        [pl.BlockSpec((rows, heads), lambda i, p: (0, 0))] * CHUNKS
        + [pl.BlockSpec(shape, lambda i, p: (0,) * len(shape))],
        [jax.ShapeDtypeStruct((rows, heads), pieces[0].dtype)] * CHUNKS
        + [jax.ShapeDtypeStruct(shape, array.dtype)],
        [],
        [*pieces, array, *released],
    )


def centred(context, resid, w_out, b_out, ln_gain, w_proj):
    row, group = lax.axis_index("dp"), lax.axis_index("groups")
    x, core = lax.axis_index("mp"), lax.axis_index("sub")
    place = jnp.stack([(row < 2).astype(jnp.int32), group, core, row, 2 * x + core, x])
    images, part, heads = context.shape
    wide, out_cols = resid.shape[2], w_proj.shape[1]
    half = wide // 2
    bias, gain = b_out.reshape(1, -1), ln_gain.reshape(1, -1)

    def inner(p):
        return 1 - p[0]

    def outer(p):
        return p[0]

    def out_block(side):
        return (w_out, (heads // 2, half), lambda i, p: (p[1], side(p)))

    def proj_block(side):
        return (w_proj, (half // 2, out_cols), lambda i, p: (2 * side(p) + p[1], 0))

    def old_block(side):
        return (resid, (images, part, half), lambda i, p: (0, 0, side(p)))

    sent, sent_outer, sent_cross = cuts(
        place,
        [
            (context, (images // 2, part, heads), lambda i, p: (1 - p[5], 0, 0)),
            out_block(outer),
            proj_block(outer),
        ],
    )
    got = along(sent, "mp", SWAP)
    fold_outer = along(sent_outer, "dp", FOLD)
    proj_cross = along(sent_cross, "dp", CROSS)

    near, away, sent_old = facing(place, context, got, old_block(outer))
    pieces = [along(near, "dp", FOLD), near, along(away, "dp", CROSS), along(away, "dp", FAR)]
    old_outer = along(sent_old, "dp", FOLD)

    sent_inner, sent_swap = cuts(
        place, [out_block(inner), (fold_outer, fold_outer.shape, None)], near
    )
    fold_inner = along(sent_inner, "dp", FOLD)
    swap_outer = along(sent_swap, "groups", SWAP)

    *own, sent_old = ordered(place, pieces, old_block(inner), sent_inner)
    old_inner = along(sent_old, "dp", FOLD)
    far = [along(v, "mp", SWAP) for v in own]
    near = [along(v, "sub", SWAP) for v in own]
    tokens_of = [(a, b, c, along(b, "sub", SWAP)) for a, b, c in zip(own, far, near)]

    def sends(k):
        weights = (w_out, fold_outer, swap_outer, resid, old_outer, bias)
        return attend(place, tokens_of[k], *weights, k, False, jnp.bfloat16)

    def keeps(k, swapped):
        weights = (w_out, fold_inner, swapped, resid, old_inner, bias)
        return attend(place, tokens_of[k], *weights, k, True, jnp.float32)

    came = [sends(0)]
    sent_far, sent_swap = cuts(
        place, [proj_block(outer), (fold_inner, fold_inner.shape, None)], came[0]
    )
    proj_far = along(sent_far, "dp", FAR)
    swap_inner = along(sent_swap, "groups", SWAP)
    came += [sends(k) for k in range(1, CHUNKS)]
    came = [along(v, "dp", CROSS) for v in came]

    kept = [keeps(k, swap_inner) for k in range(CHUNKS)]
    sent_fold, sent_swap = cuts(
        place, [proj_block(inner), (proj_cross, proj_cross.shape, None)], kept[0]
    )
    proj_fold = along(sent_fold, "dp", FOLD)
    swap_cross = along(sent_swap, "groups", SWAP)

    scaled = []
    for k in range(CHUNKS):
        near = scale_up(place, kept[k], came[k], gain)
        far = along(near, "mp", SWAP)
        scaled.append([near, along(near, "sub", SWAP), far, along(far, "sub", SWAP)])

    weights = [
        proj_fold,
        along(proj_fold, "groups", SWAP),
        proj_cross,
        swap_cross,
        proj_far,
        along(proj_far, "groups", SWAP),
    ]
    parts = []
    for k in range(CHUNKS):
        spread, own, cross, leap = project_up(place, scaled[k], w_proj, weights, gain)
        leap = along(leap, "dp", LEAP)
        cross = along(cross, "dp", CROSS)
        spread = along(spread, "dp", SPREAD)
        parts.append([own, cross, spread, leap])
    return finish(place, parts, 8 * half).reshape(1, 4 * part, out_cols)


def local(context, resid, w_out, b_out, ln_gain, w_proj):
    grid = [lax.axis_size(name) for name in ("groups", "dp", "mp", "sub")]
    fits = grid == [2, 4, 2, 2] and context.shape[0] == 4 and context.shape[1] % CHUNKS == 0
    plan = centred if fits else gathered
    return plan(context, resid, w_out, b_out, ln_gain, w_proj)


def solution(mesh):
    in_specs = (
        P("groups", "dp", ("mp", "sub")),
        P("groups", "dp", ("mp", "sub")),
        P("dp", ("mp", "sub")),
        P(("mp", "sub")),
        P(),
        P("dp", ("mp", "sub")),
    )
    out_specs = P(("groups", "dp"), None, ("mp", "sub"))
    return jax.shard_map(local, mesh=mesh, in_specs=in_specs, out_specs=out_specs, check_vma=False)
```

```python
import jax
import jax.numpy as jnp
from jax import lax
from jax.experimental import pallas as pl
from jax.experimental.pallas import tpu as pltpu
from jax.sharding import PartitionSpec as P

EPS = 1e-06
CHUNKS = 2
JOIN = 1


def normalize(values, ln_gain):
    floats = lax.optimization_barrier(values).astype(jnp.float32)
    shard_cols = values.shape[2]
    full_width = shard_cols * lax.axis_size(("mp", "sub"))
    totals, squares = lax.psum(
        (jnp.sum(floats, axis=-1, keepdims=True), jnp.sum(floats * floats, axis=-1, keepdims=True)),
        ("mp", "sub"),
    )
    center = totals / full_width
    spread = squares / full_width - center * center
    gain_share = lax.dynamic_slice_in_dim(
        ln_gain, lax.axis_index(("mp", "sub")) * shard_cols, shard_cols
    )
    shard_norm = ((floats - center) * lax.rsqrt(spread + EPS) * gain_share).astype(jnp.bfloat16)
    normed = lax.all_gather(shard_norm, ("mp", "sub"), axis=2, tiled=True)
    return normed.reshape(-1, normed.shape[2])


def project(normed, w_proj):
    summed_proj = jnp.dot(
        normed, lax.all_gather(w_proj, "dp", axis=0, tiled=True), preferred_element_type=jnp.float32
    )
    return summed_proj.astype(jnp.bfloat16)


def gathered(context, resid, w_out, b_out, ln_gain, w_proj):
    images, part_rows, head_cols = context.shape
    width_cols = resid.shape[2]
    tok_rows = context.reshape(images * part_rows, head_cols)
    heads_all = lax.all_gather(tok_rows, ("mp", "sub"), axis=1, tiled=True)
    attended = jnp.dot(
        heads_all,
        lax.all_gather(w_out, "dp", axis=0, tiled=True),
        preferred_element_type=jnp.float32,
    )
    summed = (resid.reshape(-1, width_cols).astype(jnp.float32) + attended + b_out).astype(
        jnp.bfloat16
    )
    summed = summed.reshape(images, part_rows, width_cols)
    moved = lax.all_to_all(summed, "dp", split_axis=0, concat_axis=1, tiled=True)
    normed = normalize(moved, ln_gain)
    return project(normed, w_proj).reshape(moved.shape[0], moved.shape[1], w_proj.shape[1])


SWAP = [(0, 1), (1, 0)]
FOLD = [(0, 1), (3, 2)]
CROSS = [(1, 2), (2, 1)]
FAR = [(0, 2), (3, 1)]
SPREAD = [(1, 0), (2, 3)]
LEAP = [(1, 3), (2, 0)]


def along(value, axis, pairs):
    return lax.ppermute(value, axis, pairs)


def pick(stack, index):
    return lax.dynamic_index_in_dim(stack, index, 0, keepdims=False)


def either(test, first, second):
    return jnp.where(test, first, second), jnp.where(test, second, first)


LIMIT = 32 * 1024 * 1024
ANY = pl.BlockSpec(memory_space=pl.ANY)
VMEM = pl.BlockSpec(memory_space=pltpu.VMEM)
SMEM = pl.BlockSpec(memory_space=pltpu.SMEM)
EXTRA = 16
TILE = 256


def call(kernel, place, ins, shapes, scratch, args, cost=1):
    return pl.pallas_call(
        kernel,
        in_specs=[SMEM, *ins],
        out_specs=jax.tree.map(lambda _: VMEM, shapes),
        scratch_shapes=scratch,
        out_shape=shapes,
        compiler_params=pltpu.CompilerParams(vmem_limit_bytes=LIMIT),
        cost_estimate=pl.CostEstimate(flops=cost, bytes_accessed=1, transcendentals=0),
    )(place, *args)


def shaped(shape, dtype=jnp.bfloat16):
    return jax.ShapeDtypeStruct(shape, dtype)


def moved(pairs, sems):
    copies = [pltpu.make_async_copy(src, dst, sems.at[i]) for i, (src, dst) in enumerate(pairs)]
    for copy in copies:
        copy.start()
    for copy in copies:
        copy.wait()


def cuts(place, blocks, *released, cost=1):
    def kernel(p, *refs):
        dsts = refs[-1 - len(blocks) : -1]
        pairs = [
            (src.at[at(p, block)] if at else src, dst)
            for src, dst, (_, block, at) in zip(refs, dsts, blocks)
        ]
        moved(pairs, refs[-1])

    return call(
        kernel,
        place,
        [ANY] * (len(blocks) + len(released)),
        [shaped(block, array.dtype) for array, block, _ in blocks],
        [pltpu.SemaphoreType.DMA((len(blocks),))],
        [array for array, _, _ in blocks] + list(released),
        cost,
    )


def run(index, size):
    return pl.ds(pl.multiple_of(index * size, size), size)


def terms(value):
    high = value.astype(jnp.bfloat16)
    rest = value - high.astype(jnp.float32)
    mid = rest.astype(jnp.bfloat16)
    return [high, mid, (rest - mid.astype(jnp.float32)).astype(jnp.bfloat16)]


def added(rows, first):
    high, mid, low = (rows[first + i : first + i + 1].astype(jnp.float32) for i in range(3))
    return high + (mid + low)


def packed(rows):
    parts = [term for row in rows for term in terms(row)]
    parts.append(jnp.zeros((EXTRA - len(parts), rows[0].shape[1]), jnp.bfloat16))
    return jnp.concatenate(parts, axis=0)


def upright(rows):
    rows = jnp.concatenate(rows, axis=0)
    fill = jnp.zeros((128 - rows.shape[0], rows.shape[1]), jnp.float32)
    return jnp.concatenate([rows, fill], axis=0).T


def attend(place, tokens_of, w_out, fold, swapped, resid, came, bias, part, inner, dtype):
    rows, heads = tokens_of[0].shape
    tokens = 2 * rows
    half, share = fold.shape[1], fold.shape[0]
    images, span = resid.shape[0], tokens // resid.shape[0] // 4
    tile = TILE if half % TILE == 0 else half

    def kernel(p, own, far, near, both, weight, fold, swapped, old, came, bias, out, left, total):
        low = p[0] == 1
        turn = low == (p[2] == 0)
        side = jnp.where(low == inner, 0, half)
        for at, one, two in ((p[5], own, near), (1 - p[5], far, both)):
            at = run(at, rows)
            left[at, :heads] = jnp.where(turn, two[...], one[...])
            folded = jnp.where(turn, one[...], two[...])
            first, second = folded[:, :share], folded[:, share:]
            left[at, heads : heads + share] = jnp.where(p[1] == 0, first, second)
            left[at, heads + share :] = jnp.where(p[1] == 0, second, first)
        own_at, came_at = jnp.where(low, span, 2 * span), jnp.where(low, 0, 3 * span)
        patches = slice(part * span, (part + 1) * span)
        for t in range(half // tile):
            here = slice(t * tile, (t + 1) * tile)
            there = pl.ds(pl.multiple_of(side + t * tile, tile), tile)
            value = jnp.dot(left[:, :heads], weight[:, there], preferred_element_type=jnp.float32)
            for i, piece in enumerate((fold, swapped)):
                at = slice(heads + i * share, heads + (i + 1) * share)
                value = value + jnp.dot(
                    left[:, at], piece[:, here], preferred_element_type=jnp.float32
                )
            total[...] = value + jnp.where(low, bias[:, there], 0.0)
            for image in range(images):
                for at, source, columns in ((own_at, old, there), (came_at, came, here)):
                    at = pl.ds(pl.multiple_of(image * 4 * span + at, span), span)
                    total[at, :] = total[at, :] + source[image, patches, columns].astype(
                        jnp.float32
                    )
            out[:, here] = total[...].astype(dtype)

    return call(
        kernel,
        place,
        [VMEM] * 10,
        shaped((tokens, half), dtype),
        [pltpu.VMEM((tokens, 2 * heads), jnp.bfloat16), pltpu.VMEM((tokens, tile), jnp.float32)],
        [*tokens_of, w_out, fold, swapped, resid, came, bias],
    )


def scale_up(place, keeps, came, gain, *released):
    tokens, half = keeps.shape

    def kernel(p, keeps, came, gain, *refs):
        out = refs[-1]
        scale = gain[:, run(2 * p[4] + 1 - p[0], half)]
        lane = lax.broadcasted_iota(jnp.int32, (128, 128), 1)

        def step(i):
            at = run(i, 128)
            summed = (keeps[at, :] + came[at, :].astype(jnp.float32)).astype(jnp.bfloat16)
            summed = summed.astype(jnp.float32)
            mean = jnp.sum(summed, axis=1, keepdims=True) / half
            off = summed - mean
            square = jnp.sum(off * off, axis=1, keepdims=True)
            out[at, :] = (off * scale).astype(jnp.bfloat16)
            stats = jnp.where(lane == 0, mean, jnp.where(lane == 1, square, 0.0)).T
            out[tokens:, at] = packed([stats[0:1], stats[1:2]])

        pl.loop(0, tokens // 128)(step)

    return call(
        kernel,
        place,
        [VMEM] * 3 + [ANY] * len(released),
        shaped((tokens + EXTRA, half)),
        [],
        [keeps, came, gain, *released],
    )


def project_up(place, scaled, w_proj, pieces, gain):
    rows, half = scaled[0].shape
    tokens, out_cols = rows - EXTRA, w_proj.shape[1]
    size, share = tokens // 4, half // 2
    tile = TILE if out_cols % TILE == 0 else out_cols

    def kernel(p, s0, s1, s2, s3, own, f0, f1, c0, c1, a0, a1, gain, *rest):
        outs, (left, stats, total) = rest[:4], rest[4:]
        low = p[0] == 1

        def slot(feature):
            return jnp.where(low, feature, 3 - feature)

        def put(value, at, rows):
            swap = (p[1] == 1) & (at != 1)
            first, second = value[:, :share], value[:, share:]
            left[at, rows, :share] = jnp.where(swap, second, first)
            left[at, rows, share:] = jnp.where(swap, first, second)

        last = [s[tokens:, :tokens] for s in (s0, s1, s2, s3)]
        means = [added(v, 0) for v in last]
        middle = 0.25 * (means[0] + means[1] + means[2] + means[3])
        shift = [v - middle for v in means]
        square = sum(added(v, 3) + half * (d * d) for v, d in zip(last, shift))
        for image in range(4):
            at = slice(image * size, (image + 1) * size)
            stats[image] = jnp.concatenate([middle[:, at], square[:, at]], axis=0)
        for d, s in enumerate((s0, s1, s2, s3)):
            feature = p[4] ^ d
            put(s[:tokens, :], slot(feature), slice(0, tokens))
            put(
                packed([gain[:, run(2 * feature + 1 - p[0], half)]]),
                slot(feature),
                slice(tokens, rows),
            )
        pairs = []
        for d in range(4):
            high, mid, low_term = (v.astype(jnp.float32) for v in terms(shift[d]))
            pairs += [high, high, high, mid, mid, low_term]
        shifts = upright(pairs).astype(jnp.bfloat16)

        for t in range(out_cols // tile):
            here = slice(t * tile, (t + 1) * tile)
            value = jnp.zeros((tokens, tile), jnp.float32)
            gains = []
            for at, halves in enumerate(((f0, f1), (own,), (c0, c1), (a0, a1))):
                piece = jnp.zeros((rows, tile), jnp.float32)
                if at == 1:
                    weights = [own[run(1 - p[0], half), here]]
                else:
                    weights = [weight[:, here] for weight in halves]
                for i, weight in enumerate(weights):
                    depth = weight.shape[0]
                    piece = piece + jnp.dot(
                        left[at, :, i * depth : (i + 1) * depth],
                        weight,
                        preferred_element_type=jnp.float32,
                    )
                value = value + piece[:tokens]
                gains.append(jnp.sum(piece[tokens : tokens + 3], axis=0, keepdims=True))
            fix = []
            for d in range(4):
                at = slot(p[4] ^ d)
                row = sum(jnp.where(at == i, gains[i], 0.0) for i in range(4))
                high, mid, low_term = terms(row)
                fix += [high, mid, low_term, high, mid, high]
            fix.append(jnp.zeros((128 - len(fix), tile), jnp.bfloat16))
            fix = jnp.concatenate(fix, axis=0)
            total[...] = value + jnp.dot(shifts, fix, preferred_element_type=jnp.float32)
            gains = gains[0] + gains[1] + gains[2] + gains[3]
            for role, out in enumerate(outs):
                image = jnp.where(low, role, 3 - role)
                out[:size, here] = total[run(image, size), :].astype(jnp.bfloat16)
                rest = stats[image]
                rest = jnp.concatenate([rest] * (tile // size), axis=1)
                out[size:, here] = packed([rest[0:1], rest[1:2], gains])

    return call(
        kernel,
        place,
        [VMEM] * 12,
        [shaped((size + EXTRA, out_cols))] * 4,
        [
            pltpu.VMEM((4, rows, half), jnp.bfloat16),
            pltpu.VMEM((4, 2, size), jnp.float32),
            pltpu.VMEM((tokens, tile), jnp.float32),
        ],
        [*scaled, w_proj, *pieces, gain],
    )


def finish(place, parts, count):
    rows, out_cols = parts[0][0].shape
    size = rows - EXTRA
    span = size // 4

    def kernel(p, *refs):
        out = refs[-1]
        middle = (p[3] == 1) | (p[3] == 2)
        for k in range(len(parts)):
            own, cross, spread, leap = refs[4 * k : 4 * k + 4]
            one = jnp.where(middle, own[...], spread[...])
            two = jnp.where(middle, cross[...], leap[...])
            ends = [one[size:], two[size:]]
            means = [added(v, 0)[:, :size] for v in ends]
            squares = [added(v, 3)[:, :size] for v in ends]
            gap = 0.5 * (means[0] - means[1])
            spread_of = (squares[0] + squares[1]) / count + gap * gap
            turned = upright([gap, lax.rsqrt(spread_of + EPS)])
            value = one[:size].astype(jnp.float32) + two[:size].astype(jnp.float32)
            value = value + turned[:, 0:1] * (added(ends[0], 6) - added(ends[1], 6))
            value = (value * turned[:, 1:2]).astype(jnp.bfloat16)
            for row in range(4):
                at = (row * len(parts) + k) * span
                out[at : at + span, :] = value[row * span : (row + 1) * span]

    args = [v for part in parts for v in part]
    return call(
        kernel, place, [VMEM] * len(args), shaped((size * len(parts), out_cols)), [], args
    )


def facing(place, context, got, *released):
    half_images = got.shape[0]

    def kernel(p, kept, got, *refs):
        near, away, sems = refs[-3:]
        kept = kept.at[run(p[5], half_images)]
        same = (p[0] == 1) == (p[5] == 0)

        @pl.when(same)
        def _():
            moved([(kept, near), (got, away)], sems)

        @pl.when(jnp.logical_not(same))
        def _():
            moved([(kept, away), (got, near)], sems)

    return call(
        kernel,
        place,
        [ANY] * (2 + len(released)),
        [shaped(got.shape)] * 2,
        [pltpu.SemaphoreType.DMA((2,))],
        [context, got, *released],
    )


def ordered(place, pieces, *released):
    images, part, heads = pieces[0].shape
    span = part // CHUNKS

    def kernel(p, *refs):
        ins, outs, sems = refs[:4], refs[-CHUNKS - 1 : -1], refs[-1]

        def go(ins):
            moved(
                [
                    (ins[row].at[:, k * span : (k + 1) * span], out.at[:, row])
                    for k, out in enumerate(outs)
                    for row in range(4)
                ],
                sems,
            )

        pl.when(p[0] == 1)(lambda: go(ins))
        pl.when(p[0] == 0)(lambda: go(ins[::-1]))

    outs = call(
        kernel,
        place,
        [ANY] * (4 + len(released)),
        [shaped((images, 4, span, heads))] * CHUNKS,
        [pltpu.SemaphoreType.DMA((4 * CHUNKS,))],
        [*pieces, *released],
    )
    return [v.reshape(images * 4 * span, heads) for v in outs]


def centred(context, resid, w_out, b_out, ln_gain, w_proj):
    row, group = lax.axis_index("dp"), lax.axis_index("groups")
    x, core = lax.axis_index("mp"), lax.axis_index("sub")
    place = jnp.stack([(row < 2).astype(jnp.int32), group, core, row, 2 * x + core, x])
    images, part, heads = context.shape
    wide, out_cols = resid.shape[2], w_proj.shape[1]
    half = wide // 2
    bias, gain = b_out.reshape(1, -1), ln_gain.reshape(1, -1)

    def inner(p):
        return 1 - p[0]

    def outer(p):
        return p[0]

    def out_block(side):
        shape = (heads // 2, half)
        return w_out, shape, lambda p, b: (run(p[1], b[0]), run(side(p), b[1]))

    def proj_block(side):
        shape = (half // 2, out_cols)
        return w_proj, shape, lambda p, b: (run(2 * side(p) + p[1], b[0]),)

    def old_block(side):
        shape = (images, part, half)
        return resid, shape, lambda p, b: (slice(None), slice(None), run(side(p), b[2]))

    def whole(array):
        return array, array.shape, None

    (sent,) = cuts(
        place,
        [(context, (images // 2, part, heads), lambda p, b: (run(1 - p[5], b[0]),))],
    )
    got = along(sent, "mp", SWAP)
    sent_outer, sent_cross = cuts(place, [out_block(outer), proj_block(outer)])
    fold_outer = along(sent_outer, "dp", FOLD)
    proj_cross = along(sent_cross, "dp", CROSS)

    near, away = facing(place, context, got, sent_outer)
    pieces = [along(near, "dp", FOLD), near, along(away, "dp", CROSS), along(away, "dp", FAR)]
    (sent_old,) = cuts(place, [old_block(outer)], near)
    old_outer = along(sent_old, "dp", FOLD)

    sent_inner, sent_old, sent_swap = cuts(
        place, [out_block(inner), old_block(inner), whole(fold_outer)], near
    )
    fold_inner = along(sent_inner, "dp", FOLD)
    old_inner = along(sent_old, "dp", FOLD)
    swap_outer = along(sent_swap, "groups", SWAP)

    own = ordered(place, pieces, sent_inner, proj_cross)
    far = [along(v, "mp", SWAP) for v in own]
    near = [along(v, "sub", SWAP) for v in own]
    tokens_of = [(a, b, c, along(b, "sub", SWAP)) for a, b, c in zip(own, far, near)]

    (join,) = cuts(place, [whole(swap_outer)], cost=JOIN)

    def sends(k):
        weights = (w_out, fold_outer, join, resid, old_outer, bias)
        return attend(place, tokens_of[k], *weights, k, False, jnp.bfloat16)

    def keeps(k, swapped):
        weights = (w_out, fold_inner, swapped, resid, old_inner, bias)
        return attend(place, tokens_of[k], *weights, k, True, jnp.float32)

    (sent_swap,) = cuts(place, [whole(proj_cross)], join)
    swap_cross = along(sent_swap, "groups", SWAP)
    came = [sends(0)]
    sent_far, sent_swap = cuts(place, [proj_block(outer), whole(fold_inner)], came[0])
    proj_far = along(sent_far, "dp", FAR)
    swap_inner = along(sent_swap, "groups", SWAP)
    came += [sends(k) for k in range(1, CHUNKS)]
    came = [along(v, "dp", CROSS) for v in came]

    (sent_fold,) = cuts(place, [proj_block(inner)], swap_inner)
    proj_fold = along(sent_fold, "dp", FOLD)
    kept = [keeps(k, swap_inner) for k in range(CHUNKS)]

    scaled = []
    for k in range(CHUNKS):
        near = scale_up(place, kept[k], came[k], gain, sent_fold)
        far = along(near, "mp", SWAP)
        scaled.append([near, along(near, "sub", SWAP), far, along(far, "sub", SWAP)])

    weights = [
        proj_fold,
        along(proj_fold, "groups", SWAP),
        proj_cross,
        swap_cross,
        proj_far,
        along(proj_far, "groups", SWAP),
    ]
    parts = []
    for k in range(CHUNKS):
        spread, own, cross, leap = project_up(place, scaled[k], w_proj, weights, gain)
        leap = along(leap, "dp", LEAP)
        cross = along(cross, "dp", CROSS)
        spread = along(spread, "dp", SPREAD)
        parts.append([own, cross, spread, leap])
    return finish(place, parts, 8 * half).reshape(1, 4 * part, out_cols)


def local(context, resid, w_out, b_out, ln_gain, w_proj):
    grid = [lax.axis_size(name) for name in ("groups", "dp", "mp", "sub")]
    fits = grid == [2, 4, 2, 2] and context.shape[0] == 4 and context.shape[1] % CHUNKS == 0
    plan = centred if fits else gathered
    return plan(context, resid, w_out, b_out, ln_gain, w_proj)


def solution(mesh):
    in_specs = (
        P("groups", "dp", ("mp", "sub")),
        P("groups", "dp", ("mp", "sub")),
        P("dp", ("mp", "sub")),
        P(("mp", "sub")),
        P(),
        P("dp", ("mp", "sub")),
    )
    out_specs = P(("groups", "dp"), None, ("mp", "sub"))
    return jax.shard_map(local, mesh=mesh, in_specs=in_specs, out_specs=out_specs, check_vma=False)
```

```python
import jax
import jax.numpy as jnp
from jax import lax
from jax.experimental import pallas as pl
from jax.experimental.pallas import tpu as pltpu
from jax.sharding import PartitionSpec as P

EPS = 1e-06
CHUNKS = 2
PLAN = dict(
    first=0,
    at_cross=0,
    at_old=3,
    at_inner=3,
    at_far=2,
    at_fold=3,
    due_cross=2,
    due_old=7,
    due_inner=6,
    due_far=99,
    due_fold=99,
    due_swap_cross=6,
    due_swap_far=6,
    hop_cross=0,
    hop_old=0,
    hop_inner=0,
    hop_far=0,
    hop_fold=0,
    hop_swap_cross=1,
    hop_swap_far=0,
    join=1,
    c_send=1,
    c_keep=1,
    xjoin=1,
    k3=0,
    h0=-1,
    h1=2,
    y_fold=1,
    hop_swap_fold=0,
    c_x1=1,
    c_xc=1,
    c_k3=1,
    c_ord=1,
    hop_join=-1,
    full=1,
)


def normalize(values, ln_gain):
    floats = lax.optimization_barrier(values).astype(jnp.float32)
    shard_cols = values.shape[2]
    full_width = shard_cols * lax.axis_size(("mp", "sub"))
    totals, squares = lax.psum(
        (jnp.sum(floats, axis=-1, keepdims=True), jnp.sum(floats * floats, axis=-1, keepdims=True)),
        ("mp", "sub"),
    )
    center = totals / full_width
    spread = squares / full_width - center * center
    gain_share = lax.dynamic_slice_in_dim(
        ln_gain, lax.axis_index(("mp", "sub")) * shard_cols, shard_cols
    )
    shard_norm = ((floats - center) * lax.rsqrt(spread + EPS) * gain_share).astype(jnp.bfloat16)
    normed = lax.all_gather(shard_norm, ("mp", "sub"), axis=2, tiled=True)
    return normed.reshape(-1, normed.shape[2])


def project(normed, w_proj):
    summed_proj = jnp.dot(
        normed, lax.all_gather(w_proj, "dp", axis=0, tiled=True), preferred_element_type=jnp.float32
    )
    return summed_proj.astype(jnp.bfloat16)


def gathered(context, resid, w_out, b_out, ln_gain, w_proj):
    images, part_rows, head_cols = context.shape
    width_cols = resid.shape[2]
    tok_rows = context.reshape(images * part_rows, head_cols)
    heads_all = lax.all_gather(tok_rows, ("mp", "sub"), axis=1, tiled=True)
    attended = jnp.dot(
        heads_all,
        lax.all_gather(w_out, "dp", axis=0, tiled=True),
        preferred_element_type=jnp.float32,
    )
    summed = (resid.reshape(-1, width_cols).astype(jnp.float32) + attended + b_out).astype(
        jnp.bfloat16
    )
    summed = summed.reshape(images, part_rows, width_cols)
    moved = lax.all_to_all(summed, "dp", split_axis=0, concat_axis=1, tiled=True)
    normed = normalize(moved, ln_gain)
    return project(normed, w_proj).reshape(moved.shape[0], moved.shape[1], w_proj.shape[1])


SWAP = [(0, 1), (1, 0)]
FOLD = [(0, 1), (3, 2)]
CROSS = [(1, 2), (2, 1)]
FAR = [(0, 2), (3, 1)]
SPREAD = [(1, 0), (2, 3)]
LEAP = [(1, 3), (2, 0)]


def along(value, axis, pairs):
    return lax.ppermute(value, axis, pairs)


def hop(value):
    return along(value.reshape(-1, value.shape[-1])[:16, :128], "sub", SWAP)


def hops(value, count):
    if count < 0:
        return []
    for _ in range(count):
        value = hop(value) if value.shape != (16, 128) else along(value, "sub", SWAP)
    return [value]


def pick(stack, index):
    return lax.dynamic_index_in_dim(stack, index, 0, keepdims=False)


def either(test, first, second):
    return jnp.where(test, first, second), jnp.where(test, second, first)


LIMIT = 32 * 1024 * 1024
ANY = pl.BlockSpec(memory_space=pl.ANY)
VMEM = pl.BlockSpec(memory_space=pltpu.VMEM)
SMEM = pl.BlockSpec(memory_space=pltpu.SMEM)
EXTRA = 16
TILE = 256


def call(kernel, place, ins, shapes, scratch, args, cost=1):
    return pl.pallas_call(
        kernel,
        in_specs=[SMEM, *ins],
        out_specs=jax.tree.map(lambda _: VMEM, shapes),
        scratch_shapes=scratch,
        out_shape=shapes,
        compiler_params=pltpu.CompilerParams(vmem_limit_bytes=LIMIT),
        cost_estimate=pl.CostEstimate(flops=cost, bytes_accessed=1, transcendentals=0),
    )(place, *args)


def shaped(shape, dtype=jnp.bfloat16):
    return jax.ShapeDtypeStruct(shape, dtype)


def moved(pairs, sems):
    copies = [pltpu.make_async_copy(src, dst, sems.at[i]) for i, (src, dst) in enumerate(pairs)]
    for copy in copies:
        copy.start()
    for copy in copies:
        copy.wait()


def cuts(place, outs, *released, cost=1):
    sources = [block[0] for _, blocks in outs for block in blocks]

    def kernel(p, *refs):
        dsts, sems = refs[-1 - len(outs) : -1], refs[-1]
        pairs = []
        for dst, (_, blocks) in zip(dsts, outs):
            for _, there, here in blocks:
                src = refs[len(pairs)]
                pairs.append((src.at[there(p)] if there else src, dst.at[here] if here else dst))
        moved(pairs, sems)

    return call(
        kernel,
        place,
        [ANY] * (len(sources) + len(released)),
        [shaped(shape) for shape, _ in outs],
        [pltpu.SemaphoreType.DMA((len(sources),))],
        sources + list(released),
        cost,
    )


def run(index, size):
    return pl.ds(pl.multiple_of(index * size, size), size)


def terms(value):
    high = value.astype(jnp.bfloat16)
    rest = value - high.astype(jnp.float32)
    mid = rest.astype(jnp.bfloat16)
    return [high, mid, (rest - mid.astype(jnp.float32)).astype(jnp.bfloat16)]


def added(rows, first):
    high, mid, low = (rows[first + i : first + i + 1].astype(jnp.float32) for i in range(3))
    return high + (mid + low)


def packed(rows):
    parts = [term for row in rows for term in terms(row)]
    parts.append(jnp.zeros((EXTRA - len(parts), rows[0].shape[1]), jnp.bfloat16))
    return jnp.concatenate(parts, axis=0)


def upright(rows):
    rows = jnp.concatenate(rows, axis=0)
    fill = jnp.zeros((128 - rows.shape[0], rows.shape[1]), jnp.float32)
    return jnp.concatenate([rows, fill], axis=0).T


def attend(place, tokens_of, w_out, fold, swapped, resid, others, bias, part, inner, dtype, *after, cost=1):
    rows, heads = tokens_of[0].shape
    tokens = 2 * rows
    share, half = swapped.shape
    images, patches = resid.shape[:2]
    span = tokens // images // 4
    tile = TILE if half % TILE == 0 else half

    def kernel(p, own, far, near, both, weight, fold, swapped, old, bias, *refs):
        others, (out, left, total) = refs[: -3 - len(after)], refs[-3:]
        low = p[0] == 1
        turn = low == (p[2] == 0)
        side = jnp.where(low == inner, 0, half)
        for at, one, two in ((p[5], own, near), (1 - p[5], far, both)):
            at = run(at, rows)
            left[at, :heads] = jnp.where(turn, two[...], one[...])
            folded = jnp.where(turn, one[...], two[...])
            first, second = folded[:, :share], folded[:, share:]
            left[at, heads : heads + share] = jnp.where(p[1] == 0, first, second)
            left[at, heads + share :] = jnp.where(p[1] == 0, second, first)
        row_of = [jnp.where(low, 1, 2), jnp.where(low, 0, 3), jnp.where(low, 3, 0)]
        for t in range(half // tile):
            here = slice(t * tile, (t + 1) * tile)
            there = pl.ds(pl.multiple_of(side + t * tile, tile), tile)
            value = jnp.dot(left[:, :heads], weight[:, there], preferred_element_type=jnp.float32)
            for i, piece in enumerate((fold, swapped)):
                at = slice(heads + i * share, heads + (i + 1) * share)
                value = value + jnp.dot(
                    left[:, at], piece[:share, here], preferred_element_type=jnp.float32
                )
            total[...] = value + jnp.where(low, bias[:, there], 0.0)
            for image in range(images):
                first = part * span
                more = [old[image, first : first + span, there]]
                for source in others:
                    first = source.shape[0] - (images - image) * patches + part * span
                    more.append(source[first : first + span, here])
                for row, values in zip(row_of, more):
                    at = run(image * 4 + row, span)
                    total[at, :] = total[at, :] + values.astype(jnp.float32)
            out[:, here] = total[...].astype(dtype)

    return call(
        kernel,
        place,
        [VMEM] * (9 + len(others)) + [ANY] * len(after),
        shaped((tokens, half), dtype),
        [pltpu.VMEM((tokens, 2 * heads), jnp.bfloat16), pltpu.VMEM((tokens, tile), jnp.float32)],
        [*tokens_of, w_out, fold, swapped, resid, bias, *others, *after],
        cost,
    )


def scale_up(place, keeps, came, gain, *released):
    tokens, half = keeps.shape

    def kernel(p, keeps, came, gain, *refs):
        out = refs[-1]
        scale = gain[:, run(2 * p[4] + 1 - p[0], half)]
        lane = lax.broadcasted_iota(jnp.int32, (128, 128), 1)

        def step(i):
            at = run(i, 128)
            summed = (keeps[at, :] + came[at, :].astype(jnp.float32)).astype(jnp.bfloat16)
            summed = summed.astype(jnp.float32)
            mean = jnp.sum(summed, axis=1, keepdims=True) / half
            off = summed - mean
            square = jnp.sum(off * off, axis=1, keepdims=True)
            out[at, :] = (off * scale).astype(jnp.bfloat16)
            stats = jnp.where(lane == 0, mean, jnp.where(lane == 1, square, 0.0)).T
            out[tokens:, at] = packed([stats[0:1], stats[1:2]])

        pl.loop(0, tokens // 128)(step)

    return call(
        kernel,
        place,
        [VMEM] * 3 + [ANY] * len(released),
        shaped((tokens + EXTRA, half)),
        [],
        [keeps, came, gain, *released],
    )


def project_up(place, scaled, w_proj, pieces, gain, *after):
    rows, half = scaled[0].shape
    tokens, out_cols = rows - EXTRA, w_proj.shape[1]
    size, share = tokens // 4, half // 2
    tile = TILE if out_cols % TILE == 0 else out_cols

    whole = len(pieces) % 2

    def kernel(p, s0, s1, s2, s3, own, *rest):
        fold, (c0, c1, a0, a1, gain) = rest[: 2 - whole], rest[2 - whole : 7 - whole]
        outs, (left, stats, total) = rest[-7:-3], rest[-3:]
        low = p[0] == 1

        def slot(feature):
            return jnp.where(low, feature, 3 - feature)

        def put(value, at, rows):
            swap = (p[1] == 1) & (at > 1 if whole else at != 1)
            first, second = value[:, :share], value[:, share:]
            left[at, rows, :share] = jnp.where(swap, second, first)
            left[at, rows, share:] = jnp.where(swap, first, second)

        last = [s[tokens:, :tokens] for s in (s0, s1, s2, s3)]
        means = [added(v, 0) for v in last]
        middle = 0.25 * (means[0] + means[1] + means[2] + means[3])
        shift = [v - middle for v in means]
        square = sum(added(v, 3) + half * (d * d) for v, d in zip(last, shift))
        for image in range(4):
            at = slice(image * size, (image + 1) * size)
            stats[image] = jnp.concatenate([middle[:, at], square[:, at]], axis=0)
        for d, s in enumerate((s0, s1, s2, s3)):
            feature = p[4] ^ d
            put(s[:tokens, :], slot(feature), slice(0, tokens))
            put(
                packed([gain[:, run(2 * feature + 1 - p[0], half)]]),
                slot(feature),
                slice(tokens, rows),
            )
        pairs = []
        for d in range(4):
            high, mid, low_term = (v.astype(jnp.float32) for v in terms(shift[d]))
            pairs += [high, high, high, mid, mid, low_term]
        shifts = upright(pairs).astype(jnp.bfloat16)

        for t in range(out_cols // tile):
            here = slice(t * tile, (t + 1) * tile)
            value = jnp.zeros((tokens, tile), jnp.float32)
            gains = []
            for at, halves in enumerate((fold, (own,), (c0, c1), (a0, a1))):
                piece = jnp.zeros((rows, tile), jnp.float32)
                if at == 1:
                    weights = [own[run(1 - p[0], half), here]]
                else:
                    weights = [weight[:, here] for weight in halves]
                for i, weight in enumerate(weights):
                    depth = weight.shape[0]
                    piece = piece + jnp.dot(
                        left[at, :, i * depth : (i + 1) * depth],
                        weight,
                        preferred_element_type=jnp.float32,
                    )
                value = value + piece[:tokens]
                gains.append(jnp.sum(piece[tokens : tokens + 3], axis=0, keepdims=True))
            fix = []
            for d in range(4):
                at = slot(p[4] ^ d)
                row = sum(jnp.where(at == i, gains[i], 0.0) for i in range(4))
                high, mid, low_term = terms(row)
                fix += [high, mid, low_term, high, mid, high]
            fix.append(jnp.zeros((128 - len(fix), tile), jnp.bfloat16))
            fix = jnp.concatenate(fix, axis=0)
            total[...] = value + jnp.dot(shifts, fix, preferred_element_type=jnp.float32)
            gains = gains[0] + gains[1] + gains[2] + gains[3]
            for role, out in enumerate(outs):
                image = jnp.where(low, role, 3 - role)
                out[:size, here] = total[run(image, size), :].astype(jnp.bfloat16)
                rest = stats[image]
                rest = jnp.concatenate([rest] * (tile // size), axis=1)
                out[size:, here] = packed([rest[0:1], rest[1:2], gains])

    return call(
        kernel,
        place,
        [VMEM] * (6 + len(pieces)) + [ANY] * len(after),
        [shaped((size + EXTRA, out_cols))] * 4,
        [
            pltpu.VMEM((4, rows, half), jnp.bfloat16),
            pltpu.VMEM((4, 2, size), jnp.float32),
            pltpu.VMEM((tokens, tile), jnp.float32),
        ],
        [*scaled, w_proj, *pieces, gain, *after],
    )


def finish(place, parts, count):
    rows, out_cols = parts[0][0].shape
    size = rows - EXTRA
    span = size // 4

    def kernel(p, *refs):
        out = refs[-1]
        middle = (p[3] == 1) | (p[3] == 2)
        for k in range(len(parts)):
            own, cross, spread, leap = refs[4 * k : 4 * k + 4]
            one = jnp.where(middle, own[...], spread[...])
            two = jnp.where(middle, cross[...], leap[...])
            ends = [one[size:], two[size:]]
            means = [added(v, 0)[:, :size] for v in ends]
            squares = [added(v, 3)[:, :size] for v in ends]
            gap = 0.5 * (means[0] - means[1])
            spread_of = (squares[0] + squares[1]) / count + gap * gap
            turned = upright([gap, lax.rsqrt(spread_of + EPS)])
            value = one[:size].astype(jnp.float32) + two[:size].astype(jnp.float32)
            value = value + turned[:, 0:1] * (added(ends[0], 6) - added(ends[1], 6))
            value = (value * turned[:, 1:2]).astype(jnp.bfloat16)
            for row in range(4):
                at = (row * len(parts) + k) * span
                out[at : at + span, :] = value[row * span : (row + 1) * span]

    args = [v for part in parts for v in part]
    return call(
        kernel, place, [VMEM] * len(args), shaped((size * len(parts), out_cols)), [], args
    )


def facing(place, context, got, *released):
    half_images = got.shape[0]

    def kernel(p, kept, got, *refs):
        near, away, sems = refs[-3:]
        kept = kept.at[run(p[5], half_images)]
        same = (p[0] == 1) == (p[5] == 0)

        @pl.when(same)
        def _():
            moved([(kept, near), (got, away)], sems)

        @pl.when(jnp.logical_not(same))
        def _():
            moved([(kept, away), (got, near)], sems)

    return call(
        kernel,
        place,
        [ANY] * (2 + len(released)),
        [shaped(got.shape)] * 2,
        [pltpu.SemaphoreType.DMA((2,))],
        [context, got, *released],
    )


def ordered(place, pieces, blocks, *released, cost=1):
    images, part, heads = pieces[0].shape
    span = part // CHUNKS
    sources = [block[0] for _, many in blocks for block in many]

    def kernel(p, *refs):
        ins, rest = refs[:4], refs[4 : 4 + len(sources)]
        outs, sems = refs[-1 - CHUNKS - len(blocks) : -1], refs[-1]
        more = []
        for dst, (_, many) in zip(outs[CHUNKS:], blocks):
            for _, there, here in many:
                src = rest[len(more)]
                more.append((src.at[there(p)] if there else src, dst.at[here] if here else dst))

        def go(ins):
            moved(
                [
                    (ins[row].at[:, k * span : (k + 1) * span], out.at[:, row])
                    for k, out in enumerate(outs[:CHUNKS])
                    for row in range(4)
                ]
                + more,
                sems,
            )

        pl.when(p[0] == 1)(lambda: go(ins))
        pl.when(p[0] == 0)(lambda: go(ins[::-1]))

    outs = call(
        kernel,
        place,
        [ANY] * (4 + len(sources) + len(released)),
        [shaped((images, 4, span, heads))] * CHUNKS + [shaped(shape) for shape, _ in blocks],
        [pltpu.SemaphoreType.DMA((4 * CHUNKS + len(sources),))],
        [*pieces, *sources, *released],
        cost,
    )
    return [v.reshape(images * 4 * span, heads) for v in outs[:CHUNKS]], outs[CHUNKS:]


def centred(context, resid, w_out, b_out, ln_gain, w_proj):
    row, group = lax.axis_index("dp"), lax.axis_index("groups")
    x, core = lax.axis_index("mp"), lax.axis_index("sub")
    place = jnp.stack([(row < 2).astype(jnp.int32), group, core, row, 2 * x + core, x])
    images, part, heads = context.shape
    wide, out_cols = resid.shape[2], w_proj.shape[1]
    half = wide // 2
    bias, gain = b_out.reshape(1, -1), ln_gain.reshape(1, -1)

    def inner(p):
        return 1 - p[0]

    def outer(p):
        return p[0]

    share = heads // 2, half // 2

    def out_block(side, here=None):
        return w_out, lambda p: (run(p[1], share[0]), run(side(p), half)), here

    def proj_block(side):
        return w_proj, lambda p: (run(2 * side(p) + p[1], share[1]),), None

    def old_blocks(side, start):
        return [
            (
                resid,
                lambda p, image=image: (image, slice(None), run(side(p), half)),
                (slice(start + image * part, start + (image + 1) * part),),
            )
            for image in range(images)
        ]

    out_shape, proj_shape = (share[0], half), (share[1], out_cols)

    def first(v):
        return v, lambda p: (slice(0, share[0]),), None

    old_shape = (images * part, half)

    b_swap = lambda v: (out_shape, [first(v)])
    b_cross = (proj_shape, [proj_block(outer)])
    b_far = (proj_shape, [proj_block(outer)])
    b_fold = (proj_shape, [proj_block(inner)])
    if PLAN["full"]:
        b_fold = ((half, out_cols), [(w_proj, lambda p: (run(inner(p), half),), None)])
    b_old = (old_shape, old_blocks(outer, 0))
    b_inner = (
        (share[0] + images * part, half),
        [out_block(inner, (slice(0, share[0]),)), *old_blocks(inner, share[0])],
    )
    perm = dict(cross=CROSS, far=FAR, fold=FOLD, old=FAR, inner=FOLD)
    block = dict(cross=b_cross, far=b_far, fold=b_fold, old=b_old, inner=b_inner)
    arrived = {}

    def emitted(stage):
        return [n for n in ("cross", "old", "inner", "far", "fold") if PLAN["at_" + n] == stage]

    def launch(stage, made):
        for n, v in zip(emitted(stage), made):
            arrived[n] = along(v, "dp", perm[n])

    def due(stage):
        out = []
        for n in ("cross", "old", "inner", "far", "fold", "swap_cross", "swap_far"):
            if PLAN["due_" + n] == stage and n in arrived:
                out += hops(arrived[n], PLAN["hop_" + n])
        return out

    sent = lax.dynamic_slice_in_dim(context, (1 - x) * (images // 2), images // 2, 0)
    got = along(sent, "mp", SWAP)
    sent_outer, *made = cuts(
        place,
        [(out_shape, [out_block(outer)])] + [block[n] for n in emitted(0)],
        *hops(sent, PLAN["first"]),
    )
    fold_outer = along(sent_outer, "dp", FOLD)
    launch(0, made)

    near, away = facing(place, context, got, sent_outer)
    pieces = [along(near, "dp", FOLD), near, along(away, "dp", CROSS), along(away, "dp", FAR)]
    if emitted(1):
        launch(1, cuts(place, [block[n] for n in emitted(1)], near))

    own, (sent_swap, *made) = ordered(
        place, pieces, [b_swap(fold_outer)] + [block[n] for n in emitted(2)], *due(2), cost=PLAN["c_ord"]
    )
    swap_outer = along(sent_swap, "groups", SWAP)
    launch(2, made)

    far = [along(own[0], "mp", SWAP)]
    sent, *made = cuts(
        place,
        [(own[1].shape, [(own[1], None, None)])] + [block[n] for n in emitted(3)],
        far[0],
        *due(3),
        cost=PLAN["c_x1"],
    )
    far.append(along(sent, "mp", SWAP))
    launch(3, made)
    near = [along(v, "sub", SWAP) for v in own]
    tokens_of = [(a, b, c, along(b, "sub", SWAP)) for a, b, c in zip(own, far, near)]

    (join,) = cuts(
        place, [(out_shape, [(swap_outer, None, None)])], *hops(swap_outer, PLAN["hop_join"]), cost=PLAN["join"]
    )

    def sends(k, *after):
        weights = (w_out, fold_outer, join, resid, [], bias, k, False, jnp.bfloat16)
        return attend(place, tokens_of[k], *weights, *after, cost=PLAN["c_send"])

    def keeps(k, *after):
        others = [arrived["inner"], arrived["old"]]
        weights = (w_out, arrived["inner"], swap_inner, resid, others, bias, k, True, jnp.float32)
        return attend(place, tokens_of[k], *weights, *after, cost=PLAN["c_keep"])

    (sent_swap,) = cuts(
        place, [(proj_shape, [(arrived["cross"], None, None)])], *([join] if PLAN["xjoin"] else []), cost=PLAN["c_xc"]
    )
    arrived["swap_cross"] = along(sent_swap, "groups", SWAP)
    came = [sends(0, *due(4)), sends(1, *due(5))]
    if PLAN["at_far"] < 6:
        arrived["swap_far"] = along(arrived["far"], "groups", SWAP)
    more = [came[1]] if emitted(6) or PLAN["k3"] else []
    sent_swap, *made = cuts(
        place, [b_swap(arrived["inner"])] + [block[n] for n in emitted(6)], *more, *due(6), cost=PLAN["c_k3"]
    )
    swap_inner = along(sent_swap, "groups", SWAP)
    launch(6, made)
    came = [along(v, "dp", CROSS) for v in came]

    here = [hops(v, h) for v, h in zip(came, (PLAN["h0"], PLAN["h1"]))]
    kept = [keeps(0, *due(7))]
    if emitted(7):
        launch(7, cuts(place, [block[n] for n in emitted(7)], kept[0]))
    if "swap_far" not in arrived:
        arrived["swap_far"] = along(arrived["far"], "groups", SWAP)
    kept.append(keeps(1, *due(8)))

    scaled = []
    for k in range(CHUNKS):
        near = scale_up(place, kept[k], came[k], gain, *here[k], *due(9 + k))
        far = along(near, "mp", SWAP)
        scaled.append([near, along(near, "sub", SWAP), far, along(far, "sub", SWAP)])

    sent_swap, ready = arrived["fold"], []
    if not PLAN["full"]:
        if PLAN["y_fold"] >= 0:
            (sent_swap,) = cuts(
                place, [(proj_shape, [(sent_swap, None, None)])], *hops(sent_swap, PLAN["y_fold"])
            )
        swap_fold = along(sent_swap, "groups", SWAP)
        ready = hops(swap_fold, PLAN["hop_swap_fold"])
    weights = [
        *([arrived["fold"]] if PLAN["full"] else [arrived["fold"], swap_fold]),
        arrived["cross"],
        arrived["swap_cross"],
        arrived["far"],
        arrived["swap_far"],
    ]
    ready += due(11)
    parts = []
    for k in range(CHUNKS):
        spread, own, cross, leap = project_up(place, scaled[k], w_proj, weights, gain, *ready)
        leap = along(leap, "dp", LEAP)
        cross = along(cross, "dp", CROSS)
        spread = along(spread, "dp", SPREAD)
        parts.append([own, cross, spread, leap])
    return finish(place, parts, 8 * half).reshape(1, 4 * part, out_cols)


def local(context, resid, w_out, b_out, ln_gain, w_proj):
    grid = [lax.axis_size(name) for name in ("groups", "dp", "mp", "sub")]
    fits = grid == [2, 4, 2, 2] and context.shape[0] == 4 and context.shape[1] % CHUNKS == 0
    plan = centred if fits else gathered
    return plan(context, resid, w_out, b_out, ln_gain, w_proj)


def solution(mesh):
    in_specs = (
        P("groups", "dp", ("mp", "sub")),
        P("groups", "dp", ("mp", "sub")),
        P("dp", ("mp", "sub")),
        P(("mp", "sub")),
        P(),
        P("dp", ("mp", "sub")),
    )
    out_specs = P(("groups", "dp"), None, ("mp", "sub"))
    return jax.shard_map(local, mesh=mesh, in_specs=in_specs, out_specs=out_specs, check_vma=False)
```

```python
import jax
import jax.numpy as jnp
from jax import lax
from jax.experimental import pallas as pl
from jax.experimental.pallas import tpu as pltpu
from jax.sharding import PartitionSpec as P

EPS = 1e-06
CHUNKS = 2
PLAN = dict(
    first=0,
    at_cross=2,
    at_old=3,
    at_inner=3,
    at_far=2,
    at_fold=6,
    due_cross=5,
    due_old=7,
    due_inner=6,
    due_far=4,
    due_fold=99,
    due_swap_cross=8,
    due_swap_far=6,
    hop_cross=0,
    hop_old=0,
    hop_inner=0,
    hop_far=0,
    hop_fold=0,
    hop_swap_cross=1,
    hop_swap_far=0,
    join=1,
    c_send=1,
    c_keep=1,
    xjoin=0,
    k3=0,
    h0=-1,
    h1=-1,
    y_fold=1,
    hop_swap_fold=0,
    c_x1=1,
    c_xc=1,
    c_k3=1,
    c_ord=10000000000,
    hop_join=2,
    full=1,
    hop_yi=1,
    hop_m1=0,
    hop_out=1,
)


def normalize(values, ln_gain):
    floats = lax.optimization_barrier(values).astype(jnp.float32)
    shard_cols = values.shape[2]
    full_width = shard_cols * lax.axis_size(("mp", "sub"))
    totals, squares = lax.psum(
        (jnp.sum(floats, axis=-1, keepdims=True), jnp.sum(floats * floats, axis=-1, keepdims=True)),
        ("mp", "sub"),
    )
    center = totals / full_width
    spread = squares / full_width - center * center
    gain_share = lax.dynamic_slice_in_dim(
        ln_gain, lax.axis_index(("mp", "sub")) * shard_cols, shard_cols
    )
    shard_norm = ((floats - center) * lax.rsqrt(spread + EPS) * gain_share).astype(jnp.bfloat16)
    normed = lax.all_gather(shard_norm, ("mp", "sub"), axis=2, tiled=True)
    return normed.reshape(-1, normed.shape[2])


def project(normed, w_proj):
    summed_proj = jnp.dot(
        normed, lax.all_gather(w_proj, "dp", axis=0, tiled=True), preferred_element_type=jnp.float32
    )
    return summed_proj.astype(jnp.bfloat16)


def gathered(context, resid, w_out, b_out, ln_gain, w_proj):
    images, part_rows, head_cols = context.shape
    width_cols = resid.shape[2]
    tok_rows = context.reshape(images * part_rows, head_cols)
    heads_all = lax.all_gather(tok_rows, ("mp", "sub"), axis=1, tiled=True)
    attended = jnp.dot(
        heads_all,
        lax.all_gather(w_out, "dp", axis=0, tiled=True),
        preferred_element_type=jnp.float32,
    )
    summed = (resid.reshape(-1, width_cols).astype(jnp.float32) + attended + b_out).astype(
        jnp.bfloat16
    )
    summed = summed.reshape(images, part_rows, width_cols)
    moved = lax.all_to_all(summed, "dp", split_axis=0, concat_axis=1, tiled=True)
    normed = normalize(moved, ln_gain)
    return project(normed, w_proj).reshape(moved.shape[0], moved.shape[1], w_proj.shape[1])


SWAP = [(0, 1), (1, 0)]
FOLD = [(0, 1), (3, 2)]
CROSS = [(1, 2), (2, 1)]
FAR = [(0, 2), (3, 1)]
SPREAD = [(1, 0), (2, 3)]
LEAP = [(1, 3), (2, 0)]


def along(value, axis, pairs):
    return lax.ppermute(value, axis, pairs)


def hop(value):
    return along(value.reshape(-1, value.shape[-1])[:16, :128], "sub", SWAP)


def hops(value, count):
    if count < 0:
        return []
    for _ in range(count):
        value = hop(value) if value.shape != (16, 128) else along(value, "sub", SWAP)
    return [value]


def pick(stack, index):
    return lax.dynamic_index_in_dim(stack, index, 0, keepdims=False)


def either(test, first, second):
    return jnp.where(test, first, second), jnp.where(test, second, first)


LIMIT = 32 * 1024 * 1024
ANY = pl.BlockSpec(memory_space=pl.ANY)
VMEM = pl.BlockSpec(memory_space=pltpu.VMEM)
SMEM = pl.BlockSpec(memory_space=pltpu.SMEM)
EXTRA = 16
TILE = 256


def call(kernel, place, ins, shapes, scratch, args, cost=1):
    return pl.pallas_call(
        kernel,
        in_specs=[SMEM, *ins],
        out_specs=jax.tree.map(lambda _: VMEM, shapes),
        scratch_shapes=scratch,
        out_shape=shapes,
        compiler_params=pltpu.CompilerParams(vmem_limit_bytes=LIMIT),
        cost_estimate=pl.CostEstimate(flops=cost, bytes_accessed=1, transcendentals=0),
    )(place, *args)


def shaped(shape, dtype=jnp.bfloat16):
    return jax.ShapeDtypeStruct(shape, dtype)


def moved(pairs, sems):
    copies = [pltpu.make_async_copy(src, dst, sems.at[i]) for i, (src, dst) in enumerate(pairs)]
    for copy in copies:
        copy.start()
    for copy in copies:
        copy.wait()


def cuts(place, outs, *released, cost=1):
    sources = [block[0] for _, blocks in outs for block in blocks]

    def kernel(p, *refs):
        dsts, sems = refs[-1 - len(outs) : -1], refs[-1]
        pairs = []
        for dst, (_, blocks) in zip(dsts, outs):
            for _, there, here in blocks:
                src = refs[len(pairs)]
                pairs.append((src.at[there(p)] if there else src, dst.at[here] if here else dst))
        moved(pairs, sems)

    return call(
        kernel,
        place,
        [ANY] * (len(sources) + len(released)),
        [shaped(shape) for shape, _ in outs],
        [pltpu.SemaphoreType.DMA((len(sources),))],
        sources + list(released),
        cost,
    )


def run(index, size):
    return pl.ds(pl.multiple_of(index * size, size), size)


def terms(value):
    high = value.astype(jnp.bfloat16)
    rest = value - high.astype(jnp.float32)
    mid = rest.astype(jnp.bfloat16)
    return [high, mid, (rest - mid.astype(jnp.float32)).astype(jnp.bfloat16)]


def added(rows, first):
    high, mid, low = (rows[first + i : first + i + 1].astype(jnp.float32) for i in range(3))
    return high + (mid + low)


def packed(rows):
    parts = [term for row in rows for term in terms(row)]
    parts.append(jnp.zeros((EXTRA - len(parts), rows[0].shape[1]), jnp.bfloat16))
    return jnp.concatenate(parts, axis=0)


def upright(rows):
    rows = jnp.concatenate(rows, axis=0)
    fill = jnp.zeros((128 - rows.shape[0], rows.shape[1]), jnp.float32)
    return jnp.concatenate([rows, fill], axis=0).T


def attend(place, tokens_of, w_out, fold, swapped, resid, others, bias, part, inner, dtype, *after, cost=1):
    rows, heads = tokens_of[0].shape
    tokens = 2 * rows
    share, half = swapped.shape
    images, patches = resid.shape[:2]
    span = tokens // images // 4
    tile = TILE if half % TILE == 0 else half

    def kernel(p, own, far, near, both, weight, fold, swapped, old, bias, *refs):
        others, (out, left, total) = refs[: -3 - len(after)], refs[-3:]
        low = p[0] == 1
        turn = low == (p[2] == 0)
        side = jnp.where(low == inner, 0, half)
        for at, one, two in ((p[5], own, near), (1 - p[5], far, both)):
            at = run(at, rows)
            left[at, :heads] = jnp.where(turn, two[...], one[...])
            folded = jnp.where(turn, one[...], two[...])
            first, second = folded[:, :share], folded[:, share:]
            left[at, heads : heads + share] = jnp.where(p[1] == 0, first, second)
            left[at, heads + share :] = jnp.where(p[1] == 0, second, first)
        row_of = [jnp.where(low, 1, 2), jnp.where(low, 0, 3), jnp.where(low, 3, 0)]
        for t in range(half // tile):
            here = slice(t * tile, (t + 1) * tile)
            there = pl.ds(pl.multiple_of(side + t * tile, tile), tile)
            value = jnp.dot(left[:, :heads], weight[:, there], preferred_element_type=jnp.float32)
            for i, piece in enumerate((fold, swapped)):
                at = slice(heads + i * share, heads + (i + 1) * share)
                value = value + jnp.dot(
                    left[:, at], piece[:share, here], preferred_element_type=jnp.float32
                )
            total[...] = value + jnp.where(low, bias[:, there], 0.0)
            for image in range(images):
                first = part * span
                more = [old[image, first : first + span, there]]
                for source in others:
                    first = source.shape[0] - (images - image) * patches + part * span
                    more.append(source[first : first + span, here])
                for row, values in zip(row_of, more):
                    at = run(image * 4 + row, span)
                    total[at, :] = total[at, :] + values.astype(jnp.float32)
            out[:, here] = total[...].astype(dtype)

    return call(
        kernel,
        place,
        [VMEM] * (9 + len(others)) + [ANY] * len(after),
        shaped((tokens, half), dtype),
        [pltpu.VMEM((tokens, 2 * heads), jnp.bfloat16), pltpu.VMEM((tokens, tile), jnp.float32)],
        [*tokens_of, w_out, fold, swapped, resid, bias, *others, *after],
        cost,
    )


def scale_up(place, keeps, came, gain, *released):
    tokens, half = keeps.shape

    def kernel(p, keeps, came, gain, *refs):
        out = refs[-1]
        scale = gain[:, run(2 * p[4] + 1 - p[0], half)]
        lane = lax.broadcasted_iota(jnp.int32, (128, 128), 1)

        def step(i):
            at = run(i, 128)
            summed = (keeps[at, :] + came[at, :].astype(jnp.float32)).astype(jnp.bfloat16)
            summed = summed.astype(jnp.float32)
            mean = jnp.sum(summed, axis=1, keepdims=True) / half
            off = summed - mean
            square = jnp.sum(off * off, axis=1, keepdims=True)
            out[at, :] = (off * scale).astype(jnp.bfloat16)
            stats = jnp.where(lane == 0, mean, jnp.where(lane == 1, square, 0.0)).T
            out[tokens:, at] = packed([stats[0:1], stats[1:2]])

        pl.loop(0, tokens // 128)(step)

    return call(
        kernel,
        place,
        [VMEM] * 3 + [ANY] * len(released),
        shaped((tokens + EXTRA, half)),
        [],
        [keeps, came, gain, *released],
    )


def project_up(place, scaled, w_proj, pieces, gain, *after):
    rows, half = scaled[0].shape
    tokens, out_cols = rows - EXTRA, w_proj.shape[1]
    size, share = tokens // 4, half // 2
    tile = TILE if out_cols % TILE == 0 else out_cols

    whole = len(pieces) % 2

    def kernel(p, s0, s1, s2, s3, own, *rest):
        fold, (c0, c1, a0, a1, gain) = rest[: 2 - whole], rest[2 - whole : 7 - whole]
        outs, (left, stats, total) = rest[-7:-3], rest[-3:]
        low = p[0] == 1

        def slot(feature):
            return jnp.where(low, feature, 3 - feature)

        def put(value, at, rows):
            swap = (p[1] == 1) & (at > 1 if whole else at != 1)
            first, second = value[:, :share], value[:, share:]
            left[at, rows, :share] = jnp.where(swap, second, first)
            left[at, rows, share:] = jnp.where(swap, first, second)

        last = [s[tokens:, :tokens] for s in (s0, s1, s2, s3)]
        means = [added(v, 0) for v in last]
        middle = 0.25 * (means[0] + means[1] + means[2] + means[3])
        shift = [v - middle for v in means]
        square = sum(added(v, 3) + half * (d * d) for v, d in zip(last, shift))
        for image in range(4):
            at = slice(image * size, (image + 1) * size)
            stats[image] = jnp.concatenate([middle[:, at], square[:, at]], axis=0)
        for d, s in enumerate((s0, s1, s2, s3)):
            feature = p[4] ^ d
            put(s[:tokens, :], slot(feature), slice(0, tokens))
            put(
                packed([gain[:, run(2 * feature + 1 - p[0], half)]]),
                slot(feature),
                slice(tokens, rows),
            )
        pairs = []
        for d in range(4):
            high, mid, low_term = (v.astype(jnp.float32) for v in terms(shift[d]))
            pairs += [high, high, high, mid, mid, low_term]
        shifts = upright(pairs).astype(jnp.bfloat16)

        for t in range(out_cols // tile):
            here = slice(t * tile, (t + 1) * tile)
            value = jnp.zeros((tokens, tile), jnp.float32)
            gains = []
            for at, halves in enumerate((fold, (own,), (c0, c1), (a0, a1))):
                piece = jnp.zeros((rows, tile), jnp.float32)
                if at == 1:
                    weights = [own[run(1 - p[0], half), here]]
                else:
                    weights = [weight[:, here] for weight in halves]
                for i, weight in enumerate(weights):
                    depth = weight.shape[0]
                    piece = piece + jnp.dot(
                        left[at, :, i * depth : (i + 1) * depth],
                        weight,
                        preferred_element_type=jnp.float32,
                    )
                value = value + piece[:tokens]
                gains.append(jnp.sum(piece[tokens : tokens + 3], axis=0, keepdims=True))
            fix = []
            for d in range(4):
                at = slot(p[4] ^ d)
                row = sum(jnp.where(at == i, gains[i], 0.0) for i in range(4))
                high, mid, low_term = terms(row)
                fix += [high, mid, low_term, high, mid, high]
            fix.append(jnp.zeros((128 - len(fix), tile), jnp.bfloat16))
            fix = jnp.concatenate(fix, axis=0)
            total[...] = value + jnp.dot(shifts, fix, preferred_element_type=jnp.float32)
            gains = gains[0] + gains[1] + gains[2] + gains[3]
            for role, out in enumerate(outs):
                image = jnp.where(low, role, 3 - role)
                out[:size, here] = total[run(image, size), :].astype(jnp.bfloat16)
                rest = stats[image]
                rest = jnp.concatenate([rest] * (tile // size), axis=1)
                out[size:, here] = packed([rest[0:1], rest[1:2], gains])

    return call(
        kernel,
        place,
        [VMEM] * (6 + len(pieces)) + [ANY] * len(after),
        [shaped((size + EXTRA, out_cols))] * 4,
        [
            pltpu.VMEM((4, rows, half), jnp.bfloat16),
            pltpu.VMEM((4, 2, size), jnp.float32),
            pltpu.VMEM((tokens, tile), jnp.float32),
        ],
        [*scaled, w_proj, *pieces, gain, *after],
    )


def finish(place, parts, count, *released):
    rows, out_cols = parts[0][0].shape
    size = rows - EXTRA
    span = size // 4

    def kernel(p, *refs):
        out = refs[-1]
        middle = (p[3] == 1) | (p[3] == 2)
        for k in range(len(parts)):
            own, cross, spread, leap = refs[4 * k : 4 * k + 4]
            one = jnp.where(middle, own[...], spread[...])
            two = jnp.where(middle, cross[...], leap[...])
            ends = [one[size:], two[size:]]
            means = [added(v, 0)[:, :size] for v in ends]
            squares = [added(v, 3)[:, :size] for v in ends]
            gap = 0.5 * (means[0] - means[1])
            spread_of = (squares[0] + squares[1]) / count + gap * gap
            turned = upright([gap, lax.rsqrt(spread_of + EPS)])
            value = one[:size].astype(jnp.float32) + two[:size].astype(jnp.float32)
            value = value + turned[:, 0:1] * (added(ends[0], 6) - added(ends[1], 6))
            value = (value * turned[:, 1:2]).astype(jnp.bfloat16)
            for row in range(4):
                at = (row * len(parts) + k) * span
                out[at : at + span, :] = value[row * span : (row + 1) * span]

    args = [v for part in parts for v in part]
    return call(
        kernel,
        place,
        [VMEM] * len(args) + [ANY] * len(released),
        shaped((size * len(parts), out_cols)),
        [],
        args + list(released),
    )


def facing(place, context, got, *released):
    half_images = got.shape[0]

    def kernel(p, kept, got, *refs):
        near, away, sems = refs[-3:]
        kept = kept.at[run(p[5], half_images)]
        same = (p[0] == 1) == (p[5] == 0)

        @pl.when(same)
        def _():
            moved([(kept, near), (got, away)], sems)

        @pl.when(jnp.logical_not(same))
        def _():
            moved([(kept, away), (got, near)], sems)

    return call(
        kernel,
        place,
        [ANY] * (2 + len(released)),
        [shaped(got.shape)] * 2,
        [pltpu.SemaphoreType.DMA((2,))],
        [context, got, *released],
    )


def ordered(place, pieces, blocks, *released, cost=1):
    images, part, heads = pieces[0].shape
    span = part // CHUNKS
    sources = [block[0] for _, many in blocks for block in many]

    def kernel(p, *refs):
        ins, rest = refs[:4], refs[4 : 4 + len(sources)]
        outs, sems = refs[-1 - CHUNKS - len(blocks) : -1], refs[-1]
        more = []
        for dst, (_, many) in zip(outs[CHUNKS:], blocks):
            for _, there, here in many:
                src = rest[len(more)]
                more.append((src.at[there(p)] if there else src, dst.at[here] if here else dst))

        def go(ins):
            moved(
                [
                    (ins[row].at[:, k * span : (k + 1) * span], out.at[:, row])
                    for k, out in enumerate(outs[:CHUNKS])
                    for row in range(4)
                ]
                + more,
                sems,
            )

        pl.when(p[0] == 1)(lambda: go(ins))
        pl.when(p[0] == 0)(lambda: go(ins[::-1]))

    outs = call(
        kernel,
        place,
        [ANY] * (4 + len(sources) + len(released)),
        [shaped((images, 4, span, heads))] * CHUNKS + [shaped(shape) for shape, _ in blocks],
        [pltpu.SemaphoreType.DMA((4 * CHUNKS + len(sources),))],
        [*pieces, *sources, *released],
        cost,
    )
    return [v.reshape(images * 4 * span, heads) for v in outs[:CHUNKS]], outs[CHUNKS:]


def centred(context, resid, w_out, b_out, ln_gain, w_proj):
    row, group = lax.axis_index("dp"), lax.axis_index("groups")
    x, core = lax.axis_index("mp"), lax.axis_index("sub")
    place = jnp.stack([(row < 2).astype(jnp.int32), group, core, row, 2 * x + core, x])
    images, part, heads = context.shape
    wide, out_cols = resid.shape[2], w_proj.shape[1]
    half = wide // 2
    bias, gain = b_out.reshape(1, -1), ln_gain.reshape(1, -1)

    def inner(p):
        return 1 - p[0]

    def outer(p):
        return p[0]

    share = heads // 2, half // 2

    def out_block(side, here=None):
        return w_out, lambda p: (run(p[1], share[0]), run(side(p), half)), here

    def proj_block(side):
        return w_proj, lambda p: (run(2 * side(p) + p[1], share[1]),), None

    def old_blocks(side, start):
        return [
            (
                resid,
                lambda p, image=image: (image, slice(None), run(side(p), half)),
                (slice(start + image * part, start + (image + 1) * part),),
            )
            for image in range(images)
        ]

    out_shape, proj_shape = (share[0], half), (share[1], out_cols)

    def first(v):
        return v, lambda p: (slice(0, share[0]),), None

    old_shape = (images * part, half)

    b_swap = lambda v: (out_shape, [first(v)])
    b_cross = (proj_shape, [proj_block(outer)])
    b_far = (proj_shape, [proj_block(outer)])
    b_fold = (proj_shape, [proj_block(inner)])
    if PLAN["full"]:
        b_fold = ((half, out_cols), [(w_proj, lambda p: (run(inner(p), half),), None)])
    b_old = (old_shape, old_blocks(outer, 0))
    b_inner = (
        (share[0] + images * part, half),
        [out_block(inner, (slice(0, share[0]),)), *old_blocks(inner, share[0])],
    )
    perm = dict(cross=CROSS, far=FAR, fold=FOLD, old=FAR, inner=FOLD)
    block = dict(cross=b_cross, far=b_far, fold=b_fold, old=b_old, inner=b_inner)
    arrived = {}

    def emitted(stage):
        return [n for n in ("cross", "old", "inner", "far", "fold") if PLAN["at_" + n] == stage]

    def launch(stage, made):
        for n, v in zip(emitted(stage), made):
            arrived[n] = along(v, "dp", perm[n])

    def due(stage):
        out = []
        for n in ("cross", "old", "inner", "far", "fold", "swap_cross", "swap_far"):
            if PLAN["due_" + n] == stage and n in arrived:
                out += hops(arrived[n], PLAN["hop_" + n])
        return out

    sent = lax.dynamic_slice_in_dim(context, (1 - x) * (images // 2), images // 2, 0)
    got = along(sent, "mp", SWAP)
    def opening(*released):
        return cuts(
            place,
            [(out_shape, [out_block(outer)])] + [block[n] for n in emitted(0)],
            *released,
        )

    if PLAN["first"] < 2:
        sent_outer, *made = opening(*hops(sent, PLAN["first"]))
        fold_outer = along(sent_outer, "dp", FOLD)
        launch(0, made)
        near, away = facing(place, context, got, sent_outer)
    else:
        near, away = facing(place, context, got)
        sent_outer, *made = opening(*hops(near, PLAN["first"] - 2))
        fold_outer = along(sent_outer, "dp", FOLD)
        launch(0, made)
    pieces = [along(near, "dp", FOLD), near, along(away, "dp", CROSS), along(away, "dp", FAR)]
    if emitted(1):
        launch(1, cuts(place, [block[n] for n in emitted(1)], near))

    (sent_swap,) = cuts(place, [b_swap(fold_outer)], *hops(fold_outer, PLAN["hop_m1"]))
    swap_outer = along(sent_swap, "groups", SWAP)
    own, made = ordered(
        place, pieces, [block[n] for n in emitted(2)], *due(2), cost=PLAN["c_ord"]
    )
    launch(2, made)

    far = [along(own[0], "mp", SWAP)]
    sent, *made = cuts(
        place,
        [(own[1].shape, [(own[1], None, None)])] + [block[n] for n in emitted(3)],
        far[0],
        *due(3),
        cost=PLAN["c_x1"],
    )
    far.append(along(sent, "mp", SWAP))
    launch(3, made)
    near = [along(v, "sub", SWAP) for v in own]
    tokens_of = [(a, b, c, along(b, "sub", SWAP)) for a, b, c in zip(own, far, near)]

    (join,) = cuts(
        place, [(out_shape, [(swap_outer, None, None)])], *hops(swap_outer, PLAN["hop_join"]), cost=PLAN["join"]
    )

    def sends(k, *after):
        weights = (w_out, fold_outer, join, resid, [], bias, k, False, jnp.bfloat16)
        return attend(place, tokens_of[k], *weights, *after, cost=PLAN["c_send"])

    def keeps(k, *after):
        others = [arrived["inner"], arrived["old"]]
        weights = (w_out, arrived["inner"], swap_inner, resid, others, bias, k, True, jnp.float32)
        return attend(place, tokens_of[k], *weights, *after, cost=PLAN["c_keep"])

    (sent_swap,) = cuts(
        place, [(proj_shape, [(arrived["cross"], None, None)])], *([join] if PLAN["xjoin"] else []), cost=PLAN["c_xc"]
    )
    arrived["swap_cross"] = along(sent_swap, "groups", SWAP)
    came = [sends(0, *due(4)), sends(1, *due(5))]
    if PLAN["at_far"] < 6:
        arrived["swap_far"] = along(arrived["far"], "groups", SWAP)
    more = [came[1]] if emitted(6) or PLAN["k3"] else []
    sent_swap, *made = cuts(
        place, [b_swap(arrived["inner"])] + [block[n] for n in emitted(6)], *more, *due(6), cost=PLAN["c_k3"]
    )
    swap_inner = along(sent_swap, "groups", SWAP)
    launch(6, made)
    came = [along(v, "dp", CROSS) for v in came]

    here = [hops(v, h) for v, h in zip(came, (PLAN["h0"], PLAN["h1"]))]
    yi = hops(swap_inner, PLAN["hop_yi"])
    kept = [keeps(0, *yi, *due(7))]
    if emitted(7):
        launch(7, cuts(place, [block[n] for n in emitted(7)], kept[0]))
    if "swap_far" not in arrived:
        arrived["swap_far"] = along(arrived["far"], "groups", SWAP)
    kept.append(keeps(1, *due(8)))

    scaled = []
    for k in range(CHUNKS):
        near = scale_up(place, kept[k], came[k], gain, *here[k], *due(9 + k))
        far = along(near, "mp", SWAP)
        scaled.append([near, along(near, "sub", SWAP), far, along(far, "sub", SWAP)])

    sent_swap, ready = arrived["fold"], []
    if not PLAN["full"]:
        if PLAN["y_fold"] >= 0:
            (sent_swap,) = cuts(
                place, [(proj_shape, [(sent_swap, None, None)])], *hops(sent_swap, PLAN["y_fold"])
            )
        swap_fold = along(sent_swap, "groups", SWAP)
        ready = hops(swap_fold, PLAN["hop_swap_fold"])
    weights = [
        *([arrived["fold"]] if PLAN["full"] else [arrived["fold"], swap_fold]),
        arrived["cross"],
        arrived["swap_cross"],
        arrived["far"],
        arrived["swap_far"],
    ]
    ready += due(11)
    parts, early = [], []
    for k in range(CHUNKS):
        spread, own, cross, leap = project_up(place, scaled[k], w_proj, weights, gain, *ready)
        leap = along(leap, "dp", LEAP)
        cross = along(cross, "dp", CROSS)
        spread = along(spread, "dp", SPREAD)
        parts.append([own, cross, spread, leap])
        if k < CHUNKS - 1:
            early += hops(spread, PLAN["hop_out"]) + hops(leap, PLAN["hop_out"])
    return finish(place, parts, 8 * half, *early).reshape(1, 4 * part, out_cols)


def local(context, resid, w_out, b_out, ln_gain, w_proj):
    grid = [lax.axis_size(name) for name in ("groups", "dp", "mp", "sub")]
    fits = grid == [2, 4, 2, 2] and context.shape[0] == 4 and context.shape[1] % CHUNKS == 0
    plan = centred if fits else gathered
    return plan(context, resid, w_out, b_out, ln_gain, w_proj)


def solution(mesh):
    in_specs = (
        P("groups", "dp", ("mp", "sub")),
        P("groups", "dp", ("mp", "sub")),
        P("dp", ("mp", "sub")),
        P(("mp", "sub")),
        P(),
        P("dp", ("mp", "sub")),
    )
    out_specs = P(("groups", "dp"), None, ("mp", "sub"))
    return jax.shard_map(local, mesh=mesh, in_specs=in_specs, out_specs=out_specs, check_vma=False)
```

```python
import jax
import jax.numpy as jnp
from jax import lax
from jax.experimental import pallas as pl
from jax.experimental.pallas import tpu as pltpu
from jax.sharding import PartitionSpec as P

EPS = 1e-06
CHUNKS = 2
PLAN = dict(
    first=0,
    at_cross=2,
    at_old=3,
    at_inner=3,
    at_far=2,
    at_fold=6,
    due_cross=5,
    due_old=7,
    due_inner=6,
    due_far=4,
    due_fold=99,
    due_swap_cross=8,
    due_swap_far=6,
    hop_cross=0,
    hop_old=0,
    hop_inner=0,
    hop_far=0,
    hop_fold=0,
    hop_swap_cross=1,
    hop_swap_far=0,
    join=1,
    c_send=1,
    c_keep=1,
    xjoin=0,
    k3=0,
    h0=-1,
    h1=-1,
    y_fold=1,
    hop_swap_fold=0,
    c_x1=1,
    c_xc=1,
    c_k3=1,
    c_ord=10000000000,
    hop_join=2,
    full=1,
    hop_yi=1,
    hop_m1=0,
    hop_out=1,
)


def normalize(values, ln_gain):
    floats = lax.optimization_barrier(values).astype(jnp.float32)
    shard_cols = values.shape[2]
    full_width = shard_cols * lax.axis_size(("mp", "sub"))
    totals, squares = lax.psum(
        (jnp.sum(floats, axis=-1, keepdims=True), jnp.sum(floats * floats, axis=-1, keepdims=True)),
        ("mp", "sub"),
    )
    center = totals / full_width
    spread = squares / full_width - center * center
    gain_share = lax.dynamic_slice_in_dim(
        ln_gain, lax.axis_index(("mp", "sub")) * shard_cols, shard_cols
    )
    shard_norm = ((floats - center) * lax.rsqrt(spread + EPS) * gain_share).astype(jnp.bfloat16)
    normed = lax.all_gather(shard_norm, ("mp", "sub"), axis=2, tiled=True)
    return normed.reshape(-1, normed.shape[2])


def project(normed, w_proj):
    summed_proj = jnp.dot(
        normed, lax.all_gather(w_proj, "dp", axis=0, tiled=True), preferred_element_type=jnp.float32
    )
    return summed_proj.astype(jnp.bfloat16)


def gathered(context, resid, w_out, b_out, ln_gain, w_proj):
    images, part_rows, head_cols = context.shape
    width_cols = resid.shape[2]
    tok_rows = context.reshape(images * part_rows, head_cols)
    heads_all = lax.all_gather(tok_rows, ("mp", "sub"), axis=1, tiled=True)
    attended = jnp.dot(
        heads_all,
        lax.all_gather(w_out, "dp", axis=0, tiled=True),
        preferred_element_type=jnp.float32,
    )
    summed = (resid.reshape(-1, width_cols).astype(jnp.float32) + attended + b_out).astype(
        jnp.bfloat16
    )
    summed = summed.reshape(images, part_rows, width_cols)
    moved = lax.all_to_all(summed, "dp", split_axis=0, concat_axis=1, tiled=True)
    normed = normalize(moved, ln_gain)
    return project(normed, w_proj).reshape(moved.shape[0], moved.shape[1], w_proj.shape[1])


SWAP = [(0, 1), (1, 0)]
FOLD = [(0, 1), (3, 2)]
CROSS = [(1, 2), (2, 1)]
FAR = [(0, 2), (3, 1)]
SPREAD = [(1, 0), (2, 3)]
LEAP = [(1, 3), (2, 0)]


def along(value, axis, pairs):
    return lax.ppermute(value, axis, pairs)


def hop(value):
    return along(value.reshape(-1, value.shape[-1])[:16, :128], "sub", SWAP)


def hops(value, count):
    if count < 0:
        return []
    for _ in range(count):
        value = hop(value) if value.shape != (16, 128) else along(value, "sub", SWAP)
    return [value]


def pick(stack, index):
    return lax.dynamic_index_in_dim(stack, index, 0, keepdims=False)


def either(test, first, second):
    return jnp.where(test, first, second), jnp.where(test, second, first)


LIMIT = 32 * 1024 * 1024
ANY = pl.BlockSpec(memory_space=pl.ANY)
VMEM = pl.BlockSpec(memory_space=pltpu.VMEM)
SMEM = pl.BlockSpec(memory_space=pltpu.SMEM)
EXTRA = 16
TILE = 512


def call(kernel, place, ins, shapes, scratch, args, cost=1):
    return pl.pallas_call(
        kernel,
        in_specs=[SMEM, *ins],
        out_specs=jax.tree.map(lambda _: VMEM, shapes),
        scratch_shapes=scratch,
        out_shape=shapes,
        compiler_params=pltpu.CompilerParams(vmem_limit_bytes=LIMIT),
        cost_estimate=pl.CostEstimate(flops=cost, bytes_accessed=1, transcendentals=0),
    )(place, *args)


def shaped(shape, dtype=jnp.bfloat16):
    return jax.ShapeDtypeStruct(shape, dtype)


def moved(pairs, sems):
    copies = [pltpu.make_async_copy(src, dst, sems.at[i]) for i, (src, dst) in enumerate(pairs)]
    for copy in copies:
        copy.start()
    for copy in copies:
        copy.wait()


def cuts(place, outs, *released, cost=1):
    sources = [block[0] for _, blocks in outs for block in blocks]

    def kernel(p, *refs):
        dsts, sems = refs[-1 - len(outs) : -1], refs[-1]
        pairs = []
        for dst, (_, blocks) in zip(dsts, outs):
            for _, there, here in blocks:
                src = refs[len(pairs)]
                pairs.append((src.at[there(p)] if there else src, dst.at[here] if here else dst))
        moved(pairs, sems)

    return call(
        kernel,
        place,
        [ANY] * (len(sources) + len(released)),
        [shaped(shape) for shape, _ in outs],
        [pltpu.SemaphoreType.DMA((len(sources),))],
        sources + list(released),
        cost,
    )


def run(index, size):
    return pl.ds(pl.multiple_of(index * size, size), size)


def terms(value):
    high = value.astype(jnp.bfloat16)
    rest = value - high.astype(jnp.float32)
    mid = rest.astype(jnp.bfloat16)
    return [high, mid, (rest - mid.astype(jnp.float32)).astype(jnp.bfloat16)]


def added(rows, first):
    high, mid, low = (rows[first + i : first + i + 1].astype(jnp.float32) for i in range(3))
    return high + (mid + low)


def packed(rows):
    parts = [term for row in rows for term in terms(row)]
    parts.append(jnp.zeros((EXTRA - len(parts), rows[0].shape[1]), jnp.bfloat16))
    return jnp.concatenate(parts, axis=0)


def upright(rows):
    rows = jnp.concatenate(rows, axis=0)
    fill = jnp.zeros((128 - rows.shape[0], rows.shape[1]), jnp.float32)
    return jnp.concatenate([rows, fill], axis=0).T


def attend(place, tokens_of, w_out, fold, swapped, resid, others, bias, part, inner, dtype, *after, cost=1):
    rows, heads = tokens_of[0].shape
    tokens = 2 * rows
    share, half = swapped.shape
    images, patches = resid.shape[:2]
    span = tokens // images // 4
    tile = TILE if half % TILE == 0 else half

    def kernel(p, own, far, near, both, weight, fold, swapped, old, bias, *refs):
        others, (out, left, total) = refs[: -3 - len(after)], refs[-3:]
        low = p[0] == 1
        turn = low == (p[2] == 0)
        side = jnp.where(low == inner, 0, half)
        for at, one, two in ((p[5], own, near), (1 - p[5], far, both)):
            at = run(at, rows)
            left[at, :heads] = jnp.where(turn, two[...], one[...])
            folded = jnp.where(turn, one[...], two[...])
            first, second = folded[:, :share], folded[:, share:]
            left[at, heads : heads + share] = jnp.where(p[1] == 0, first, second)
            left[at, heads + share :] = jnp.where(p[1] == 0, second, first)
        row_of = [jnp.where(low, 1, 2), jnp.where(low, 0, 3), jnp.where(low, 3, 0)]
        for t in range(half // tile):
            here = slice(t * tile, (t + 1) * tile)
            there = pl.ds(pl.multiple_of(side + t * tile, tile), tile)
            value = jnp.dot(left[:, :heads], weight[:, there], preferred_element_type=jnp.float32)
            for i, piece in enumerate((fold, swapped)):
                at = slice(heads + i * share, heads + (i + 1) * share)
                value = value + jnp.dot(
                    left[:, at], piece[:share, here], preferred_element_type=jnp.float32
                )
            total[...] = value + jnp.where(low, bias[:, there], 0.0)
            for image in range(images):
                first = part * span
                more = [old[image, first : first + span, there]]
                for source in others:
                    first = source.shape[0] - (images - image) * patches + part * span
                    more.append(source[first : first + span, here])
                for row, values in zip(row_of, more):
                    at = run(image * 4 + row, span)
                    total[at, :] = total[at, :] + values.astype(jnp.float32)
            out[:, here] = total[...].astype(dtype)

    return call(
        kernel,
        place,
        [VMEM] * (9 + len(others)) + [ANY] * len(after),
        shaped((tokens, half), dtype),
        [pltpu.VMEM((tokens, 2 * heads), jnp.bfloat16), pltpu.VMEM((tokens, tile), jnp.float32)],
        [*tokens_of, w_out, fold, swapped, resid, bias, *others, *after],
        cost,
    )


def scale_up(place, keeps, came, gain, *released):
    tokens, half = keeps.shape

    def kernel(p, keeps, came, gain, *refs):
        out = refs[-1]
        scale = gain[:, run(2 * p[4] + 1 - p[0], half)]
        lane = lax.broadcasted_iota(jnp.int32, (128, 128), 1)

        def step(i):
            at = run(i, 128)
            summed = (keeps[at, :] + came[at, :].astype(jnp.float32)).astype(jnp.bfloat16)
            summed = summed.astype(jnp.float32)
            mean = jnp.sum(summed, axis=1, keepdims=True) / half
            off = summed - mean
            square = jnp.sum(off * off, axis=1, keepdims=True)
            out[at, :] = (off * scale).astype(jnp.bfloat16)
            stats = jnp.where(lane == 0, mean, jnp.where(lane == 1, square, 0.0)).T
            out[tokens:, at] = packed([stats[0:1], stats[1:2]])

        pl.loop(0, tokens // 128)(step)

    return call(
        kernel,
        place,
        [VMEM] * 3 + [ANY] * len(released),
        shaped((tokens + EXTRA, half)),
        [],
        [keeps, came, gain, *released],
    )


def project_up(place, scaled, w_proj, pieces, gain, *after):
    rows, half = scaled[0].shape
    tokens, out_cols = rows - EXTRA, w_proj.shape[1]
    size, share = tokens // 4, half // 2
    tile = TILE if out_cols % TILE == 0 else out_cols

    whole = len(pieces) % 2

    def kernel(p, s0, s1, s2, s3, own, *rest):
        fold, (c0, c1, a0, a1, gain) = rest[: 2 - whole], rest[2 - whole : 7 - whole]
        outs, (left, stats, total) = rest[-7:-3], rest[-3:]
        low = p[0] == 1

        def slot(feature):
            return jnp.where(low, feature, 3 - feature)

        def put(value, at, rows):
            swap = (p[1] == 1) & (at > 1 if whole else at != 1)
            first, second = value[:, :share], value[:, share:]
            left[at, rows, :share] = jnp.where(swap, second, first)
            left[at, rows, share:] = jnp.where(swap, first, second)

        last = [s[tokens:, :tokens] for s in (s0, s1, s2, s3)]
        means = [added(v, 0) for v in last]
        middle = 0.25 * (means[0] + means[1] + means[2] + means[3])
        shift = [v - middle for v in means]
        square = sum(added(v, 3) + half * (d * d) for v, d in zip(last, shift))
        for image in range(4):
            at = slice(image * size, (image + 1) * size)
            stats[image] = jnp.concatenate([middle[:, at], square[:, at]], axis=0)
        for d, s in enumerate((s0, s1, s2, s3)):
            feature = p[4] ^ d
            put(s[:tokens, :], slot(feature), slice(0, tokens))
            put(
                packed([gain[:, run(2 * feature + 1 - p[0], half)]]),
                slot(feature),
                slice(tokens, rows),
            )
        pairs = []
        for d in range(4):
            high, mid, low_term = (v.astype(jnp.float32) for v in terms(shift[d]))
            pairs += [high, high, high, mid, mid, low_term]
        shifts = upright(pairs).astype(jnp.bfloat16)

        for t in range(out_cols // tile):
            here = slice(t * tile, (t + 1) * tile)
            value = jnp.zeros((tokens, tile), jnp.float32)
            gains = []
            for at, halves in enumerate((fold, (own,), (c0, c1), (a0, a1))):
                piece = jnp.zeros((rows, tile), jnp.float32)
                if at == 1:
                    weights = [own[run(1 - p[0], half), here]]
                else:
                    weights = [weight[:, here] for weight in halves]
                for i, weight in enumerate(weights):
                    depth = weight.shape[0]
                    piece = piece + jnp.dot(
                        left[at, :, i * depth : (i + 1) * depth],
                        weight,
                        preferred_element_type=jnp.float32,
                    )
                value = value + piece[:tokens]
                gains.append(jnp.sum(piece[tokens : tokens + 3], axis=0, keepdims=True))
            fix = []
            for d in range(4):
                at = slot(p[4] ^ d)
                row = sum(jnp.where(at == i, gains[i], 0.0) for i in range(4))
                high, mid, low_term = terms(row)
                fix += [high, mid, low_term, high, mid, high]
            fix.append(jnp.zeros((128 - len(fix), tile), jnp.bfloat16))
            fix = jnp.concatenate(fix, axis=0)
            total[...] = value + jnp.dot(shifts, fix, preferred_element_type=jnp.float32)
            gains = gains[0] + gains[1] + gains[2] + gains[3]
            for role, out in enumerate(outs):
                image = jnp.where(low, role, 3 - role)
                out[:size, here] = total[run(image, size), :].astype(jnp.bfloat16)
                rest = stats[image]
                rest = jnp.concatenate([rest] * (tile // size), axis=1)
                out[size:, here] = packed([rest[0:1], rest[1:2], gains])

    return call(
        kernel,
        place,
        [VMEM] * (6 + len(pieces)) + [ANY] * len(after),
        [shaped((size + EXTRA, out_cols))] * 4,
        [
            pltpu.VMEM((4, rows, half), jnp.bfloat16),
            pltpu.VMEM((4, 2, size), jnp.float32),
            pltpu.VMEM((tokens, tile), jnp.float32),
        ],
        [*scaled, w_proj, *pieces, gain, *after],
    )


def finish(place, parts, count, *released):
    rows, out_cols = parts[0][0].shape
    size = rows - EXTRA
    span = size // 4

    def kernel(p, *refs):
        out = refs[-1]
        middle = (p[3] == 1) | (p[3] == 2)
        for k in range(len(parts)):
            own, cross, spread, leap = refs[4 * k : 4 * k + 4]
            one = jnp.where(middle, own[...], spread[...])
            two = jnp.where(middle, cross[...], leap[...])
            ends = [one[size:], two[size:]]
            means = [added(v, 0)[:, :size] for v in ends]
            squares = [added(v, 3)[:, :size] for v in ends]
            gap = 0.5 * (means[0] - means[1])
            spread_of = (squares[0] + squares[1]) / count + gap * gap
            turned = upright([gap, lax.rsqrt(spread_of + EPS)])
            value = one[:size].astype(jnp.float32) + two[:size].astype(jnp.float32)
            value = value + turned[:, 0:1] * (added(ends[0], 6) - added(ends[1], 6))
            value = (value * turned[:, 1:2]).astype(jnp.bfloat16)
            for row in range(4):
                at = (row * len(parts) + k) * span
                out[at : at + span, :] = value[row * span : (row + 1) * span]

    args = [v for part in parts for v in part]
    return call(
        kernel,
        place,
        [VMEM] * len(args) + [ANY] * len(released),
        shaped((size * len(parts), out_cols)),
        [],
        args + list(released),
    )


def facing(place, context, got, *released):
    half_images = got.shape[0]

    def kernel(p, kept, got, *refs):
        near, away, sems = refs[-3:]
        kept = kept.at[run(p[5], half_images)]
        same = (p[0] == 1) == (p[5] == 0)

        @pl.when(same)
        def _():
            moved([(kept, near), (got, away)], sems)

        @pl.when(jnp.logical_not(same))
        def _():
            moved([(kept, away), (got, near)], sems)

    return call(
        kernel,
        place,
        [ANY] * (2 + len(released)),
        [shaped(got.shape)] * 2,
        [pltpu.SemaphoreType.DMA((2,))],
        [context, got, *released],
    )


def ordered(place, pieces, blocks, *released, cost=1):
    images, part, heads = pieces[0].shape
    span = part // CHUNKS
    sources = [block[0] for _, many in blocks for block in many]

    def kernel(p, *refs):
        ins, rest = refs[:4], refs[4 : 4 + len(sources)]
        outs, sems = refs[-1 - CHUNKS - len(blocks) : -1], refs[-1]
        more = []
        for dst, (_, many) in zip(outs[CHUNKS:], blocks):
            for _, there, here in many:
                src = rest[len(more)]
                more.append((src.at[there(p)] if there else src, dst.at[here] if here else dst))

        def go(ins):
            moved(
                [
                    (ins[row].at[:, k * span : (k + 1) * span], out.at[:, row])
                    for k, out in enumerate(outs[:CHUNKS])
                    for row in range(4)
                ]
                + more,
                sems,
            )

        pl.when(p[0] == 1)(lambda: go(ins))
        pl.when(p[0] == 0)(lambda: go(ins[::-1]))

    outs = call(
        kernel,
        place,
        [ANY] * (4 + len(sources) + len(released)),
        [shaped((images, 4, span, heads))] * CHUNKS + [shaped(shape) for shape, _ in blocks],
        [pltpu.SemaphoreType.DMA((4 * CHUNKS + len(sources),))],
        [*pieces, *sources, *released],
        cost,
    )
    return [v.reshape(images * 4 * span, heads) for v in outs[:CHUNKS]], outs[CHUNKS:]


def centred(context, resid, w_out, b_out, ln_gain, w_proj):
    row, group = lax.axis_index("dp"), lax.axis_index("groups")
    x, core = lax.axis_index("mp"), lax.axis_index("sub")
    place = jnp.stack([(row < 2).astype(jnp.int32), group, core, row, 2 * x + core, x])
    images, part, heads = context.shape
    wide, out_cols = resid.shape[2], w_proj.shape[1]
    half = wide // 2
    bias, gain = b_out.reshape(1, -1), ln_gain.reshape(1, -1)

    def inner(p):
        return 1 - p[0]

    def outer(p):
        return p[0]

    share = heads // 2, half // 2

    def out_block(side, here=None):
        return w_out, lambda p: (run(p[1], share[0]), run(side(p), half)), here

    def proj_block(side):
        return w_proj, lambda p: (run(2 * side(p) + p[1], share[1]),), None

    def old_blocks(side, start):
        return [
            (
                resid,
                lambda p, image=image: (image, slice(None), run(side(p), half)),
                (slice(start + image * part, start + (image + 1) * part),),
            )
            for image in range(images)
        ]

    out_shape, proj_shape = (share[0], half), (share[1], out_cols)

    def first(v):
        return v, lambda p: (slice(0, share[0]),), None

    old_shape = (images * part, half)

    b_swap = lambda v: (out_shape, [first(v)])
    b_cross = (proj_shape, [proj_block(outer)])
    b_far = (proj_shape, [proj_block(outer)])
    b_fold = (proj_shape, [proj_block(inner)])
    if PLAN["full"]:
        b_fold = ((half, out_cols), [(w_proj, lambda p: (run(inner(p), half),), None)])
    b_old = (old_shape, old_blocks(outer, 0))
    b_inner = (
        (share[0] + images * part, half),
        [out_block(inner, (slice(0, share[0]),)), *old_blocks(inner, share[0])],
    )
    perm = dict(cross=CROSS, far=FAR, fold=FOLD, old=FAR, inner=FOLD)
    block = dict(cross=b_cross, far=b_far, fold=b_fold, old=b_old, inner=b_inner)
    arrived = {}

    def emitted(stage):
        return [n for n in ("cross", "old", "inner", "far", "fold") if PLAN["at_" + n] == stage]

    def launch(stage, made):
        for n, v in zip(emitted(stage), made):
            arrived[n] = along(v, "dp", perm[n])

    def due(stage):
        out = []
        for n in ("cross", "old", "inner", "far", "fold", "swap_cross", "swap_far"):
            if PLAN["due_" + n] == stage and n in arrived:
                out += hops(arrived[n], PLAN["hop_" + n])
        return out

    sent = lax.dynamic_slice_in_dim(context, (1 - x) * (images // 2), images // 2, 0)
    got = along(sent, "mp", SWAP)
    def opening(*released):
        return cuts(
            place,
            [(out_shape, [out_block(outer)])] + [block[n] for n in emitted(0)],
            *released,
        )

    if PLAN["first"] < 2:
        sent_outer, *made = opening(*hops(sent, PLAN["first"]))
        fold_outer = along(sent_outer, "dp", FOLD)
        launch(0, made)
        near, away = facing(place, context, got, sent_outer)
    else:
        near, away = facing(place, context, got)
        sent_outer, *made = opening(*hops(near, PLAN["first"] - 2))
        fold_outer = along(sent_outer, "dp", FOLD)
        launch(0, made)
    pieces = [along(near, "dp", FOLD), near, along(away, "dp", CROSS), along(away, "dp", FAR)]
    if emitted(1):
        launch(1, cuts(place, [block[n] for n in emitted(1)], near))

    (sent_swap,) = cuts(place, [b_swap(fold_outer)], *hops(fold_outer, PLAN["hop_m1"]))
    swap_outer = along(sent_swap, "groups", SWAP)
    own, made = ordered(
        place, pieces, [block[n] for n in emitted(2)], *due(2), cost=PLAN["c_ord"]
    )
    launch(2, made)

    far = [along(own[0], "mp", SWAP)]
    sent, *made = cuts(
        place,
        [(own[1].shape, [(own[1], None, None)])] + [block[n] for n in emitted(3)],
        far[0],
        *due(3),
        cost=PLAN["c_x1"],
    )
    far.append(along(sent, "mp", SWAP))
    launch(3, made)
    near = [along(v, "sub", SWAP) for v in own]
    tokens_of = [(a, b, c, along(b, "sub", SWAP)) for a, b, c in zip(own, far, near)]

    (join,) = cuts(
        place, [(out_shape, [(swap_outer, None, None)])], *hops(swap_outer, PLAN["hop_join"]), cost=PLAN["join"]
    )

    def sends(k, *after):
        weights = (w_out, fold_outer, join, resid, [], bias, k, False, jnp.bfloat16)
        return attend(place, tokens_of[k], *weights, *after, cost=PLAN["c_send"])

    def keeps(k, *after):
        others = [arrived["inner"], arrived["old"]]
        weights = (w_out, arrived["inner"], swap_inner, resid, others, bias, k, True, jnp.float32)
        return attend(place, tokens_of[k], *weights, *after, cost=PLAN["c_keep"])

    (sent_swap,) = cuts(
        place, [(proj_shape, [(arrived["cross"], None, None)])], *([join] if PLAN["xjoin"] else []), cost=PLAN["c_xc"]
    )
    arrived["swap_cross"] = along(sent_swap, "groups", SWAP)
    came = [sends(0, *due(4)), sends(1, *due(5))]
    if PLAN["at_far"] < 6:
        arrived["swap_far"] = along(arrived["far"], "groups", SWAP)
    more = [came[1]] if emitted(6) or PLAN["k3"] else []
    sent_swap, *made = cuts(
        place, [b_swap(arrived["inner"])] + [block[n] for n in emitted(6)], *more, *due(6), cost=PLAN["c_k3"]
    )
    swap_inner = along(sent_swap, "groups", SWAP)
    launch(6, made)
    came = [along(v, "dp", CROSS) for v in came]

    here = [hops(v, h) for v, h in zip(came, (PLAN["h0"], PLAN["h1"]))]
    yi = hops(swap_inner, PLAN["hop_yi"])
    kept = [keeps(0, *yi, *due(7))]
    if emitted(7):
        launch(7, cuts(place, [block[n] for n in emitted(7)], kept[0]))
    if "swap_far" not in arrived:
        arrived["swap_far"] = along(arrived["far"], "groups", SWAP)
    kept.append(keeps(1, *due(8)))

    scaled = []
    for k in range(CHUNKS):
        near = scale_up(place, kept[k], came[k], gain, *here[k], *due(9 + k))
        far = along(near, "mp", SWAP)
        scaled.append([near, along(near, "sub", SWAP), far, along(far, "sub", SWAP)])

    sent_swap, ready = arrived["fold"], []
    if not PLAN["full"]:
        if PLAN["y_fold"] >= 0:
            (sent_swap,) = cuts(
                place, [(proj_shape, [(sent_swap, None, None)])], *hops(sent_swap, PLAN["y_fold"])
            )
        swap_fold = along(sent_swap, "groups", SWAP)
        ready = hops(swap_fold, PLAN["hop_swap_fold"])
    weights = [
        *([arrived["fold"]] if PLAN["full"] else [arrived["fold"], swap_fold]),
        arrived["cross"],
        arrived["swap_cross"],
        arrived["far"],
        arrived["swap_far"],
    ]
    ready += due(11)
    parts, early = [], []
    for k in range(CHUNKS):
        spread, own, cross, leap = project_up(place, scaled[k], w_proj, weights, gain, *ready)
        leap = along(leap, "dp", LEAP)
        cross = along(cross, "dp", CROSS)
        spread = along(spread, "dp", SPREAD)
        parts.append([own, cross, spread, leap])
        if k < CHUNKS - 1:
            early += hops(spread, PLAN["hop_out"]) + hops(leap, PLAN["hop_out"])
    return finish(place, parts, 8 * half, *early).reshape(1, 4 * part, out_cols)


def local(context, resid, w_out, b_out, ln_gain, w_proj):
    grid = [lax.axis_size(name) for name in ("groups", "dp", "mp", "sub")]
    fits = grid == [2, 4, 2, 2] and context.shape[0] == 4 and context.shape[1] % CHUNKS == 0
    plan = centred if fits else gathered
    return plan(context, resid, w_out, b_out, ln_gain, w_proj)


def solution(mesh):
    in_specs = (
        P("groups", "dp", ("mp", "sub")),
        P("groups", "dp", ("mp", "sub")),
        P("dp", ("mp", "sub")),
        P(("mp", "sub")),
        P(),
        P("dp", ("mp", "sub")),
    )
    out_specs = P(("groups", "dp"), None, ("mp", "sub"))
    return jax.shard_map(local, mesh=mesh, in_specs=in_specs, out_specs=out_specs, check_vma=False)
```
